256 devices in a mesh: depth: 32 (over y, z), rows: 8 (over x, core).
Axes of the slice: x: 4, y: 4, z: 8, core: 2. Of those that a mesh axis runs over, the one named last changes fastest.
Arguments:
- density_raw: bfloat16 [1024, 128, 1024], P('depth', 'rows'), may hold values from -6 to 6
- colour_raw: bfloat16 [3, 1024, 128, 1024], P(None, 'depth', 'rows'), may hold values from -6 to 6
- target: float32 [3, 128, 1024], P(None, 'rows'), may hold values from 0 to 1
- slab_rank: int32 [32], replicated, may hold values from 0 to 31, each once
Outputs:
- grad_density: float32 [1024, 128, 1024], P('depth', 'rows')
- grad_colour: float32 [3, 1024, 128, 1024], P(None, 'depth', 'rows')
The draws below stay inside these ranges and needn't reach their ends.
Inputs may be any that keep to these rules, and one draw needn't show every extreme that they name: slab_rank is a permutation: every slab has its own position along the rays.
All inputs are finite; a program needn't handle non-finite values.
Results may differ from the reference program's by a relative error of at most 0.0003.
Values may be sent and summed in bfloat16 or wider, within the bound.
A program may use at most 128 MiB of HBM per device.

```python
import jax
import jax.numpy as jnp
from jax import lax

SLICES_DEV = 32
WIDTH = 1024
SLICES = 1024
IMAGE_ROWS = 128
SLABS = 32


def levels(own_key, dims, pieces, least, high):
    def one(axis_at, parts):
        heights = jax.random.uniform(jax.random.fold_in(jax.random.fold_in(own_key, 6), axis_at), (parts,), jnp.float32, least / len(pieces), high / len(pieces))
        return jnp.repeat(jnp.exp(heights), dims[axis_at] // parts).reshape((-1,) + (1,) * (len(dims) - axis_at - 1))

    level = one(*pieces[0])
    for cut in pieces[1:]:
        level = level * one(*cut)
    return level


def gaussian(rng, dims, spread, most, shards=(), held_as=jnp.bfloat16):
    loudness = levels(rng, dims, shards, -0.22, 0.18) if shards else 1.0
    array = jax.random.normal(rng, dims, jnp.float32) * spread * loudness
    return jnp.minimum(jnp.maximum(array, -most), most).astype(held_as)


def setup_inputs(seed: int = 0) -> dict:
    seeds = jax.random.split(jax.random.key(seed), 5)
    return {
        "density_raw": gaussian(seeds[0], (SLICES, IMAGE_ROWS, WIDTH), 1.0, 6.0, ((0, 32), (1, 8))),
        "colour_raw": gaussian(seeds[1], (3, SLICES, IMAGE_ROWS, WIDTH), 1.0, 6.0, ((1, 32), (2, 8))),
        "target": jnp.clip(1.0 * jax.random.uniform(seeds[2], (3, IMAGE_ROWS, WIDTH), jnp.float32) ** levels(seeds[2], (3, IMAGE_ROWS, WIDTH), ((1, 8),), -0.2, 0.2), 0.0, 1.0),
        "slab_rank": jax.random.permutation(seeds[3], SLABS).astype(jnp.int32),
    }


optical_depth = 2.5
smooth_weight = 0.05


def along_rays(matrix, values):
    shape = values.shape
    flat = values.reshape(shape[0], shape[1], -1)
    mixed = jnp.einsum("ij,cjp->cip", matrix, flat, precision=lax.Precision.HIGHEST)
    return mixed.reshape(shape)


def triangles(count):
    index = jnp.arange(count, dtype=jnp.int32)
    before = (index[None, :] < index[:, None]).astype(jnp.float32)
    after = (index[None, :] > index[:, None]).astype(jnp.float32)
    return before, after


def slab_terms(density, colour_raw, step_depth):
    dense = density.astype(jnp.float32)
    colour = jax.nn.sigmoid(colour_raw.astype(jnp.float32))
    depth_term = step_depth * jax.nn.softplus(dense)
    opacity = -jnp.expm1(-depth_term)
    kept = jnp.exp(-depth_term)
    before, after = triangles(dense.shape[0])
    front_light = jnp.exp(-along_rays(before, depth_term[None]))[0]
    through = front_light * kept
    passing = jnp.exp(-jnp.sum(depth_term, axis=0))
    weighted = front_light[None] * opacity[None] * colour
    behind_local = along_rays(after, weighted) / through[None]
    after_light = passing[None] / through
    partial_value = jnp.concatenate([jnp.sum(weighted, axis=1), passing[None]], axis=0)
    return partial_value, (dense, colour, opacity, behind_local, after_light, front_light)


def slab_gradients(saved, scaled_residual, scaled_behind, slices_total):
    dense, colour, opacity, behind_local, after_light, front_light = saved
    lit = front_light * opacity
    grad_colour = slices_total * scaled_residual[:, None] * lit[None] * colour * (1.0 - colour)
    inner = jnp.sum(scaled_residual[:, None] * (colour - behind_local), axis=0) - after_light * scaled_behind[None]
    grad_density = optical_depth * front_light * (1.0 - opacity) * jax.nn.sigmoid(dense) * inner
    return grad_density, grad_colour


def composite(partials, slab_rank, target_piece):
    count = partials.shape[1]
    one_hot = (slab_rank[:, None] == jnp.arange(count, dtype=jnp.int32)[None]).astype(partials.dtype)
    ordered = jnp.einsum("sk,csl->ckl", one_hot, partials, precision=lax.Precision.HIGHEST)
    emitted, kept = ordered[:3], ordered[3:]
    before, after = triangles(count)
    front = jnp.exp(along_rays(before, jnp.log(kept)))
    weighted = front * emitted
    behind = along_rays(after, weighted) / (front * kept)
    residual = jnp.sum(weighted, axis=1) - target_piece
    scaled_residual = front * residual[:, None]
    scaled_behind = front * jnp.sum(residual[:, None] * behind, axis=0, keepdims=True)
    stacked = jnp.concatenate([scaled_residual, scaled_behind], axis=0)
    return jnp.einsum("sk,ckl->csl", one_hot, stacked, precision=lax.Precision.HIGHEST)


def smooth_gradient(dense):
    along_z = dense[1:] - dense[:-1]
    along_y = dense[:, 1:] - dense[:, :-1]
    grad_z = jnp.pad(along_z, ((1, 0), (0, 0), (0, 0))) - jnp.pad(along_z, ((0, 1), (0, 0), (0, 0)))
    grad_y = jnp.pad(along_y, ((0, 0), (1, 0), (0, 0))) - jnp.pad(along_y, ((0, 0), (0, 1), (0, 0)))
    return 2.0 * smooth_weight * (grad_z + grad_y)


def reference(density_raw, colour_raw, target, slab_rank):
    step_depth = optical_depth / SLICES
    dens_slabs = density_raw.reshape(SLABS, SLICES_DEV, IMAGE_ROWS, WIDTH)
    colour_slabs = jnp.moveaxis(colour_raw.reshape(3, SLABS, SLICES_DEV, IMAGE_ROWS, WIDTH), 1, 0)

    def forward(item):
        return slab_terms(item[0], item[1], step_depth)[0]

    partial_all = lax.map(forward, (dens_slabs, colour_slabs))
    partials = jnp.moveaxis(partial_all, 0, 1).reshape(4, SLABS, IMAGE_ROWS * WIDTH)
    returned = composite(partials, slab_rank, target.reshape(3, IMAGE_ROWS * WIDTH))
    returned = jnp.moveaxis(returned.reshape(4, SLABS, IMAGE_ROWS, WIDTH), 1, 0)

    def backward(item):
        partial_value, saved = slab_terms(item[0], item[1], step_depth)
        return slab_gradients(saved, item[2][:3], item[2][3], SLICES)

    grad_dens, grad_col = lax.map(backward, (dens_slabs, colour_slabs, returned))
    grad_density = grad_dens.reshape(SLICES, IMAGE_ROWS, WIDTH) + smooth_gradient(density_raw.astype(jnp.float32))
    grad_colour = jnp.moveaxis(grad_col, 0, 1).reshape(3, SLICES, IMAGE_ROWS, WIDTH)
    return grad_density, grad_colour
```

```python
import functools

import jax
import jax.numpy as jnp
from jax import lax
from jax.experimental import pallas as pl
from jax.experimental.pallas import tpu as pltpu
from jax.sharding import PartitionSpec as P

optical_depth = 2.5
smooth_weight = 0.05

LANES = 128
BAND_ROWS = 4
UNROLL = 8


def remote(src, dst, send_sem, recv_sem, axis, peer):
    return pltpu.make_async_remote_copy(
        src_ref=src,
        dst_ref=dst,
        send_sem=send_sem,
        recv_sem=recv_sem,
        device_id={axis: peer},
        device_id_type=pl.DeviceIdType.MESH,
    )


def light_kernel(
    slabs,
    groups,
    dens_hbm,
    colour_hbm,
    target_hbm,
    rank_ref,
    colour_out,
    lit_out,
    through_out,
    slope_out,
    smooth_out,
    answer_out,
    dens,
    colour_in,
    target_in,
    edge,
    edge_sent,
    rim_got,
    rim,
    partial_sent,
    partial_got,
    answer_sent,
    answer_got,
    dens_sem,
    colour_sem,
    target_sem,
    send_sem,
    recv_sem,
    rim_send_sem,
    rim_recv_sem,
):
    depth_at = lax.axis_index("depth")
    rows_at = lax.axis_index("rows")
    slices, rows, width = dens_hbm.shape
    blocks = width // LANES
    bands = rows // BAND_ROWS
    message = 4 * BAND_ROWS
    slices_total = slices * slabs
    step_depth = optical_depth / slices_total
    first_block = lax.rem(depth_at // bands + blocks // 2, blocks)

    def lanes_of(block):
        return pl.ds(pl.multiple_of(block * LANES, LANES), LANES)

    def rows_of(slab):
        return pl.ds(pl.multiple_of(slab * message, message), message)

    def input_copies(block):
        lanes = lanes_of(block)
        return (
            pltpu.make_async_copy(
                dens_hbm.at[:, :, lanes], dens.at[pl.ds(1, slices), :, lanes], dens_sem.at[block]
            ),
            pltpu.make_async_copy(
                colour_hbm.at[:, :, :, lanes], colour_in.at[:, :, :, lanes], colour_sem.at[block]
            ),
        )

    def start_inputs(k, _):
        for copy in input_copies(lax.rem(first_block + k, blocks)):
            copy.start()
        return 0

    lax.fori_loop(0, blocks, start_inputs, 0)
    my_block = depth_at // bands
    target_copy = pltpu.make_async_copy(
        target_hbm.at[:, :, lanes_of(my_block)], target_in, target_sem
    )
    target_copy.start()

    barrier = pltpu.get_barrier_semaphore()

    def greet(j, _):
        pl.semaphore_signal(
            barrier,
            inc=1,
            device_id={"depth": lax.rem(depth_at + j, slabs)},
            device_id_type=pl.DeviceIdType.MESH,
        )
        return 0

    lax.fori_loop(1, slabs, greet, 0)
    rows_up = lax.rem(rows_at + 1, groups)
    rows_down = lax.rem(rows_at + groups - 1, groups)
    depth_up = lax.rem(depth_at + 1, slabs)
    depth_down = lax.rem(depth_at + slabs - 1, slabs)
    for peer in (rows_up, rows_down):
        pl.semaphore_signal(
            barrier, inc=1, device_id={"rows": peer}, device_id_type=pl.DeviceIdType.MESH
        )

    slice_up = remote(
        dens_hbm.at[slices - 1], dens.at[0], rim_send_sem.at[0], rim_recv_sem.at[0], "depth", depth_up
    )
    slice_down = remote(
        dens_hbm.at[0],
        dens.at[slices + 1],
        rim_send_sem.at[1],
        rim_recv_sem.at[1],
        "depth",
        depth_down,
    )
    row_up = remote(
        edge_sent.at[1], rim_got.at[0], rim_send_sem.at[2], rim_recv_sem.at[2], "rows", rows_up
    )
    row_down = remote(
        edge_sent.at[0], rim_got.at[1], rim_send_sem.at[3], rim_recv_sem.at[3], "rows", rows_down
    )

    def partial_copy(owner):
        return remote(
            partial_sent.at[rows_of(owner)],
            partial_got.at[rows_of(depth_at)],
            send_sem.at[0],
            recv_sem.at[0],
            "depth",
            owner,
        )

    def forward_block(k, _):
        block = lax.rem(first_block + k, blocks)
        lanes = lanes_of(block)
        for copy in input_copies(block):
            copy.wait()

        def forward_step(step, carry):
            total, light, *shine = carry
            firsts, lasts = ([], [])
            for u in range(UNROLL):
                z = step * UNROLL + u
                x = dens[z + 1, :, lanes].astype(jnp.float32)
                firsts.append(x[:1])
                lasts.append(x[rows - 1 :])
                d = step_depth * jnp.log(1.0 + jnp.exp(x))
                opacity = d * (1.0 - d * (0.5 - d * (1.0 / 6.0 - d * (1.0 / 24.0))))
                lit = light * opacity
                total = total + d
                light = light - lit
                lit_out[z, :, lanes] = lit
                through_out[z, :, lanes] = light
                for c in range(3):
                    raw = colour_in[c, z, :, lanes].astype(jnp.float32)
                    colour = 1.0 / (1.0 + jnp.exp(-raw))
                    colour_out[c, z, :, lanes] = colour
                    shine[c] = shine[c] + lit * colour
            chunk = pl.ds(pl.multiple_of(step * UNROLL, UNROLL), UNROLL)
            edge[0, chunk, lanes] = jnp.concatenate(firsts, axis=0)
            edge[1, chunk, lanes] = jnp.concatenate(lasts, axis=0)
            return (total, light, *shine)

        zero = jnp.zeros((rows, LANES), jnp.float32)
        total, _, *shine = lax.fori_loop(
            0, slices // UNROLL, forward_step, (zero, zero + 1.0, zero, zero, zero)
        )
        base = pl.multiple_of(block * (bands * message), bands * message)
        for g in range(bands):
            for c, value in enumerate((*shine, total)):
                partial_sent[pl.ds(base + g * message + c * BAND_ROWS, BAND_ROWS), :] = value[
                    g * BAND_ROWS : (g + 1) * BAND_ROWS
                ]

        @pl.when(k == 0)
        def _():
            pl.semaphore_wait(barrier, slabs + 1)
            slice_up.start()
            slice_down.start()

        for g in range(bands):
            owner = block * bands + lax.rem(depth_at + g, bands)

            @pl.when(owner != depth_at)
            def _():
                partial_copy(owner).start()

        return 0

    lax.fori_loop(0, blocks, forward_block, 0)
    partial_got[rows_of(depth_at), :] = partial_sent[rows_of(depth_at), :]
    edge_sent[...] = edge[...].astype(jnp.bfloat16)
    row_up.start()
    row_down.start()

    ranks_row = jnp.zeros((slabs, LANES), jnp.int32)
    ranks_column = jnp.zeros((slabs, LANES), jnp.int32)
    lane = lax.broadcasted_iota(jnp.int32, (slabs, LANES), 1)
    sub = lax.broadcasted_iota(jnp.int32, (slabs, LANES), 0)
    for s in range(slabs):
        rank = rank_ref[s]
        ranks_row = jnp.where(lane == s, rank, ranks_row)
        ranks_column = jnp.where(sub == s, rank, ranks_column)
    earlier = (ranks_row < ranks_column).astype(jnp.float32)[:, :slabs]
    onward = (ranks_row >= ranks_column).astype(jnp.float32)[:, :slabs]

    def slope_block(block, _):
        lanes = lanes_of(block)

        def slope_step(step, _):
            for u in range(UNROLL):
                z = step * UNROLL + u
                x = dens[z + 1, :, lanes].astype(jnp.float32)
                slope_out[z, :, lanes] = optical_depth / (1.0 + jnp.exp(-x))
            return 0

        return lax.fori_loop(0, slices // UNROLL, slope_step, 0)

    lax.fori_loop(0, blocks, slope_block, 0)
    target_copy.wait()

    others = pl.ds(0, (slabs - 1) * message)
    pltpu.make_async_copy(partial_got.at[others], partial_got.at[others], recv_sem.at[0]).wait()

    def gathered(c):
        return jnp.concatenate(
            [
                partial_got[pl.ds(c * BAND_ROWS + j, slabs, stride=message), :]
                for j in range(BAND_ROWS)
            ],
            axis=1,
        )

    def mixed(matrix, value):
        return jnp.dot(
            matrix,
            value,
            precision=lax.Precision.HIGHEST,
            preferred_element_type=jnp.float32,
        )

    front = jnp.exp(-mixed(earlier, gathered(3)))
    band_row = lax.rem(depth_at, bands) * BAND_ROWS
    glow = jnp.zeros_like(front)
    answers = []
    for c in range(3):
        weighted = front * gathered(c)
        goal = jnp.concatenate(
            [target_in[c, pl.ds(band_row + j, 1), :] for j in range(BAND_ROWS)], axis=1
        )
        residual = jnp.sum(weighted, axis=0, keepdims=True) - goal
        glow = glow + residual * weighted
        answers.append(front * residual)
    answers.append(mixed(onward, glow))
    for c, value in enumerate(answers):
        for j in range(BAND_ROWS):
            answer_sent[pl.ds(c * BAND_ROWS + j, slabs, stride=message), :] = value[
                :, j * LANES : (j + 1) * LANES
            ]

    def answer_copy(slab):
        return remote(
            answer_sent.at[rows_of(slab)],
            answer_got.at[rows_of(depth_at)],
            send_sem.at[1],
            recv_sem.at[1],
            "depth",
            slab,
        )

    def answer_start(j, _):
        answer_copy(lax.rem(depth_at + j + slabs // 2, slabs)).start()
        return 0

    lax.fori_loop(0, slabs // 2, answer_start, 0)
    lax.fori_loop(slabs // 2 + 1, slabs, answer_start, 0)
    answer_got[rows_of(depth_at), :] = answer_sent[rows_of(depth_at), :]

    for copy in (slice_up, slice_down, row_up, row_down):
        copy.wait()

    @pl.when(depth_at == 0)
    def _():
        dens[0] = dens[1]

    @pl.when(depth_at == slabs - 1)
    def _():
        dens[slices + 1] = dens[slices]

    rim[...] = rim_got[...].astype(jnp.float32)

    @pl.when(rows_at == 0)
    def _():
        rim[0] = edge[0]

    @pl.when(rows_at == groups - 1)
    def _():
        rim[1] = edge[1]

    def smooth_block(block, _):
        lanes = lanes_of(block)
        row = lax.broadcasted_iota(jnp.int32, (rows, LANES), 0)

        def smooth_step(step, carry):
            low, centre = carry
            chunk = pl.ds(pl.multiple_of(step * UNROLL, UNROLL), UNROLL)
            above, below = (rim[0, chunk, lanes], rim[1, chunk, lanes])
            for u in range(UNROLL):
                z = step * UNROLL + u
                high = dens[z + 2, :, lanes].astype(jnp.float32)
                upper = jnp.where(row == 0, above[u : u + 1], pltpu.roll(centre, 1, axis=0))
                lower = jnp.where(
                    row == rows - 1, below[u : u + 1], pltpu.roll(centre, rows - 1, axis=0)
                )
                smooth_out[z, :, lanes] = (2.0 * smooth_weight) * (
                    (centre - low) + (centre - high) + (centre - upper) + (centre - lower)
                )
                low, centre = centre, high
            return low, centre

        start = (dens[0, :, lanes].astype(jnp.float32), dens[1, :, lanes].astype(jnp.float32))
        lax.fori_loop(0, slices // UNROLL, smooth_step, start)
        return 0

    lax.fori_loop(0, blocks, smooth_block, 0)

    pltpu.make_async_copy(answer_got.at[others], answer_got.at[others], recv_sem.at[1]).wait()
    answer_out[...] = answer_got[...]
    pltpu.make_async_copy(partial_sent.at[others], partial_sent.at[others], send_sem.at[0]).wait()
    pltpu.make_async_copy(answer_sent.at[others], answer_sent.at[others], send_sem.at[1]).wait()


def gradient_kernel(
    slices_total,
    colour_ref,
    lit_ref,
    through_ref,
    slope_ref,
    smooth_ref,
    answer_ref,
    dens_grad_hbm,
    colour_grad_hbm,
    dens_grad,
    colour_grad,
    dens_sem,
    colour_sem,
):
    slices, rows, width = lit_ref.shape
    blocks = width // LANES
    bands = rows // BAND_ROWS
    message = 4 * BAND_ROWS

    def output_copies(block):
        lanes = pl.ds(pl.multiple_of(block * LANES, LANES), LANES)
        return (
            pltpu.make_async_copy(
                dens_grad.at[:, :, lanes], dens_grad_hbm.at[:, :, lanes], dens_sem.at[block]
            ),
            pltpu.make_async_copy(
                colour_grad.at[:, :, :, lanes],
                colour_grad_hbm.at[:, :, :, lanes],
                colour_sem.at[block],
            ),
        )

    def gradient_block(block, _):
        lanes = pl.ds(pl.multiple_of(block * LANES, LANES), LANES)
        base = pl.multiple_of(block * (bands * message), bands * message)

        def answer(c):
            return jnp.concatenate(
                [
                    answer_ref[pl.ds(base + g * message + c * BAND_ROWS, BAND_ROWS), :]
                    for g in range(bands)
                ],
                axis=0,
            )

        residual = [answer(c) for c in range(3)]
        strong = [slices_total * value for value in residual]

        def gradient_step(step, remaining):
            for u in range(UNROLL):
                z = step * UNROLL + u
                lit = lit_ref[z, :, lanes]
                seen = jnp.zeros_like(lit)
                for c in range(3):
                    colour = colour_ref[c, z, :, lanes]
                    seen = seen + residual[c] * colour
                    colour_grad[c, z, :, lanes] = (strong[c] * lit) * (colour * (1.0 - colour))
                remaining = remaining - lit * seen
                dens_grad[z, :, lanes] = (
                    slope_ref[z, :, lanes] * (through_ref[z, :, lanes] * seen - remaining)
                    + smooth_ref[z, :, lanes]
                )
            return remaining

        lax.fori_loop(0, slices // UNROLL, gradient_step, answer(3))
        for copy in output_copies(block):
            copy.start()
        return 0

    lax.fori_loop(0, blocks, gradient_block, 0)

    def finish(block, _):
        for copy in output_copies(block):
            copy.wait()
        return 0

    lax.fori_loop(0, blocks, finish, 0)


def local(slabs, groups, density_raw, colour_raw, target, slab_rank):
    slices, rows, width = density_raw.shape
    blocks = width // LANES
    message = 4 * BAND_ROWS
    voxels = (slices, rows, width)
    f32 = jnp.float32
    bf16 = jnp.bfloat16
    anywhere = pl.BlockSpec(memory_space=pl.ANY)
    vmem = pl.BlockSpec(memory_space=pltpu.VMEM)
    packet = pltpu.VMEM((slabs * message, LANES), f32)
    saved = pl.pallas_call(
        functools.partial(light_kernel, slabs, groups),
        out_shape=(
            pltpu.VMEM((3, *voxels), f32),
            pltpu.VMEM(voxels, f32),
            pltpu.VMEM(voxels, f32),
            pltpu.VMEM(voxels, f32),
            pltpu.VMEM(voxels, f32),
            packet,
        ),
        in_specs=[anywhere, anywhere, anywhere, pl.BlockSpec(memory_space=pltpu.SMEM)],
        out_specs=(vmem,) * 6,
        scratch_shapes=[
            pltpu.VMEM((slices + 2, rows, width), bf16),
            pltpu.VMEM((3, *voxels), bf16),
            pltpu.VMEM((3, rows, LANES), f32),
            pltpu.VMEM((2, slices, width), f32),
            pltpu.VMEM((2, slices, width), bf16),
            pltpu.VMEM((2, slices, width), bf16),
            pltpu.VMEM((2, slices, width), f32),
            packet,
            packet,
            packet,
            packet,
            pltpu.SemaphoreType.DMA((blocks,)),
            pltpu.SemaphoreType.DMA((blocks,)),
            pltpu.SemaphoreType.DMA,
            pltpu.SemaphoreType.DMA((2,)),
            pltpu.SemaphoreType.DMA((2,)),
            pltpu.SemaphoreType.DMA((4,)),
            pltpu.SemaphoreType.DMA((4,)),
        ],
        compiler_params=pltpu.CompilerParams(
            collective_id=0, has_side_effects=True, vmem_limit_bytes=40 * 2**20
        ),
        name="light",
    )(density_raw, colour_raw, target, slab_rank)
    return pl.pallas_call(
        functools.partial(gradient_kernel, float(slices * slabs)),
        out_shape=(
            jax.ShapeDtypeStruct(voxels, f32),
            jax.ShapeDtypeStruct((3, *voxels), f32),
        ),
        in_specs=[vmem] * 6,
        out_specs=(anywhere, anywhere),
        scratch_shapes=[
            pltpu.VMEM(voxels, f32),
            pltpu.VMEM((3, *voxels), f32),
            pltpu.SemaphoreType.DMA((blocks,)),
            pltpu.SemaphoreType.DMA((blocks,)),
        ],
        compiler_params=pltpu.CompilerParams(vmem_limit_bytes=16 * 2**20),
        name="gradient",
    )(*saved)


def solution(mesh):
    return jax.shard_map(
        functools.partial(local, mesh.shape["depth"], mesh.shape["rows"]),
        mesh=mesh,
        in_specs=(P("depth", "rows", None), P(None, "depth", "rows", None), P(None, "rows", None), P()),
        out_specs=(P("depth", "rows", None), P(None, "depth", "rows", None)),
        check_vma=False,
    )
```

```python
import functools
import math

import jax
import jax.numpy as jnp
from jax import lax
from jax.experimental import pallas as pl
from jax.experimental.pallas import tpu as pltpu
from jax.sharding import PartitionSpec as P

optical_depth = 2.5
smooth_weight = 0.05

LANES = 128
BAND_ROWS = 4
UNROLL = 8
RAW_LIMIT = 6.0
CODE_TOP = 32767.0
ANSWER_KNEE = 2.0**-10


def log_code(least, most):
    low, high = (math.log(least) - 1e-3, math.log(most) + 1e-3)
    return (0.5 * (low + high), 2.0 * CODE_TOP / (high - low))


def partial_codes(slices, slices_total):
    soft = (math.log1p(math.exp(-RAW_LIMIT)), math.log1p(math.exp(RAW_LIMIT)))
    span = optical_depth / slices_total * slices
    blocked = [-math.expm1(-span * value) for value in soft]
    colour = [1.0 / (1.0 + math.exp(sign * RAW_LIMIT)) for sign in (1, -1)]
    return [log_code(*colour)] * 3 + [log_code(*blocked)]


def answer_scales():
    return [math.asinh(top / ANSWER_KNEE) / CODE_TOP for top in (1.001, 1.001, 1.001, 3.01)]


def to_code(value):
    kept = jnp.clip(value, -CODE_TOP, CODE_TOP)
    return jnp.floor(kept + 0.5)


def from_log_code(code, middle, scale):
    return jnp.exp(code * (1.0 / scale) + middle)


def to_answer_code(value, scale):
    tall = jnp.abs(value) * (1.0 / ANSWER_KNEE)
    code = jnp.log(tall + jnp.sqrt(tall * tall + 1.0)) * (1.0 / scale)
    return to_code(jnp.where(value < 0.0, -code, code))


def from_answer_code(code, scale):
    grown = jnp.exp(code * scale)
    return (0.5 * ANSWER_KNEE) * (grown - 1.0 / grown)


def far_first(k, count):
    return lax.rem(count // 2 + (2 * (k % 2) - 1) * ((k + 1) // 2) + count, count)


def as_words(code):
    return code.astype(jnp.int32).astype(jnp.int16)


def as_floats(words):
    return words.astype(jnp.int32).astype(jnp.float32)


def remote(src, dst, send_sem, recv_sem, axis, peer):
    return pltpu.make_async_remote_copy(
        src_ref=src,
        dst_ref=dst,
        send_sem=send_sem,
        recv_sem=recv_sem,
        device_id={axis: peer},
        device_id_type=pl.DeviceIdType.MESH,
    )


def light_kernel(
    slabs,
    groups,
    dens_hbm,
    colour_hbm,
    target_hbm,
    rank_ref,
    colour_out,
    lit_out,
    through_out,
    slope_out,
    smooth_out,
    mean_out,
    answer_out,
    dens,
    colour_in,
    target_in,
    edge,
    edge_sent,
    rim_got,
    rim,
    partial_sent,
    partial_got,
    answer_sent,
    answer_got,
    codes,
    dens_sem,
    colour_sem,
    target_sem,
    send_sem,
    recv_sem,
    rim_send_sem,
    rim_recv_sem,
):
    depth_at = lax.axis_index("depth")
    rows_at = lax.axis_index("rows")
    slices, rows, width = dens_hbm.shape
    blocks = width // LANES
    bands = rows // BAND_ROWS
    message = 4 * BAND_ROWS
    slices_total = slices * slabs
    step_depth = optical_depth / slices_total
    my_block = lax.rem(depth_at, blocks)
    my_band = depth_at // blocks
    codings = partial_codes(slices, slices_total)

    def lanes_of(block):
        return pl.ds(pl.multiple_of(block * LANES, LANES), LANES)

    def rows_of(slab):
        return pl.ds(pl.multiple_of(slab * message, message), message)

    def input_copies(block):
        lanes = lanes_of(block)
        return (
            pltpu.make_async_copy(
                dens_hbm.at[:, :, lanes], dens.at[pl.ds(1, slices), :, lanes], dens_sem.at[block]
            ),
            pltpu.make_async_copy(
                colour_hbm.at[:, :, :, lanes], colour_in.at[:, :, :, lanes], colour_sem.at[block]
            ),
        )

    def block_at(k):
        return lax.rem(my_block + far_first(k, blocks), blocks)

    def owner_at(block, g):
        return lax.rem(my_band + far_first(g, bands), bands) * blocks + block

    def start_inputs(k, _):
        for copy in input_copies(block_at(k)):
            copy.start()
        return 0

    lax.fori_loop(0, blocks, start_inputs, 0)
    target_copy = pltpu.make_async_copy(
        target_hbm.at[:, :, lanes_of(my_block)], target_in, target_sem
    )
    target_copy.start()

    barrier = pltpu.get_barrier_semaphore()

    def greet(j, _):
        pl.semaphore_signal(
            barrier,
            inc=1,
            device_id={"depth": lax.rem(depth_at + j, slabs)},
            device_id_type=pl.DeviceIdType.MESH,
        )
        return 0

    lax.fori_loop(1, slabs, greet, 0)
    rows_up = lax.rem(rows_at + 1, groups)
    rows_down = lax.rem(rows_at + groups - 1, groups)
    depth_up = lax.rem(depth_at + 1, slabs)
    depth_down = lax.rem(depth_at + slabs - 1, slabs)
    for peer in (rows_up, rows_down):
        pl.semaphore_signal(
            barrier, inc=1, device_id={"rows": peer}, device_id_type=pl.DeviceIdType.MESH
        )

    slice_up = remote(
        dens_hbm.at[slices - 1], dens.at[0], rim_send_sem.at[0], rim_recv_sem.at[0], "depth", depth_up
    )
    slice_down = remote(
        dens_hbm.at[0],
        dens.at[slices + 1],
        rim_send_sem.at[1],
        rim_recv_sem.at[1],
        "depth",
        depth_down,
    )
    row_up = remote(
        edge_sent.at[1], rim_got.at[0], rim_send_sem.at[2], rim_recv_sem.at[2], "rows", rows_up
    )
    row_down = remote(
        edge_sent.at[0], rim_got.at[1], rim_send_sem.at[3], rim_recv_sem.at[3], "rows", rows_down
    )

    def partial_copy(owner):
        return remote(
            partial_sent.at[rows_of(owner)],
            partial_got.at[rows_of(depth_at)],
            send_sem.at[0],
            recv_sem.at[0],
            "depth",
            owner,
        )

    def forward_block(k, _):
        block = block_at(k)
        lanes = lanes_of(block)
        for copy in input_copies(block):
            copy.wait()

        def forward_step(step, carry):
            blocked, light, *shine = carry
            firsts, lasts = ([], [])
            for u in range(UNROLL):
                z = step * UNROLL + u
                x = dens[z + 1, :, lanes].astype(jnp.float32)
                firsts.append(x[:1])
                lasts.append(x[rows - 1 :])
                d = step_depth * jnp.log(1.0 + jnp.exp(x))
                opacity = d * (1.0 - d * (0.5 - d * (1.0 / 6.0 - d * (1.0 / 24.0))))
                lit = light * opacity
                blocked = blocked + lit
                light = light - lit
                lit_out[z, :, lanes] = lit
                through_out[z, :, lanes] = light
                for c in range(3):
                    raw = colour_in[c, z, :, lanes].astype(jnp.float32)
                    colour = 1.0 / (1.0 + jnp.exp(-raw))
                    colour_out[c, z, :, lanes] = colour
                    shine[c] = shine[c] + lit * colour
            chunk = pl.ds(pl.multiple_of(step * UNROLL, UNROLL), UNROLL)
            edge[0, chunk, lanes] = jnp.concatenate(firsts, axis=0)
            edge[1, chunk, lanes] = jnp.concatenate(lasts, axis=0)
            return (blocked, light, *shine)

        zero = jnp.zeros((rows, LANES), jnp.float32)
        blocked, light, *shine = lax.fori_loop(
            0, slices // UNROLL, forward_step, (zero, zero + 1.0, zero, zero, zero)
        )
        mean = [value / blocked for value in shine]
        for c in range(3):
            mean_out[c, :, lanes] = shine[c] + light * mean[c]
        mean_out[3, :, lanes] = light
        coded = [
            to_code((jnp.log(value) - middle) * scale)
            for value, (middle, scale) in zip((*mean, blocked), codings)
        ]
        for g in range(bands):
            packed = [value[g * BAND_ROWS : (g + 1) * BAND_ROWS] for value in coded]
            partial_sent[rows_of(g * blocks + block), :] = as_words(
                jnp.concatenate(packed, axis=0)
            )

        @pl.when(k == 0)
        def _():
            pl.semaphore_wait(barrier, slabs + 1)
            slice_up.start()
            slice_down.start()

        for g in range(bands):
            owner = owner_at(block, g)

            @pl.when(owner != depth_at)
            def _():
                partial_copy(owner).start()

        return 0

    lax.fori_loop(0, blocks, forward_block, 0)
    partial_got[rows_of(depth_at), :] = partial_sent[rows_of(depth_at), :]
    edge_sent[...] = edge[...].astype(jnp.bfloat16)
    row_up.start()
    row_down.start()

    ranks_row = jnp.zeros((slabs, LANES), jnp.int32)
    ranks_column = jnp.zeros((slabs, LANES), jnp.int32)
    lane = lax.broadcasted_iota(jnp.int32, (slabs, LANES), 1)
    sub = lax.broadcasted_iota(jnp.int32, (slabs, LANES), 0)
    for s in range(slabs):
        rank = rank_ref[s]
        ranks_row = jnp.where(lane == s, rank, ranks_row)
        ranks_column = jnp.where(sub == s, rank, ranks_column)
    earlier = (ranks_row < ranks_column).astype(jnp.float32)[:, :slabs]
    later = (ranks_row > ranks_column).astype(jnp.float32)[:, :slabs]

    def slope_block(block, _):
        lanes = lanes_of(block)

        def slope_step(step, _):
            for u in range(UNROLL):
                z = step * UNROLL + u
                x = dens[z + 1, :, lanes].astype(jnp.float32)
                slope_out[z, :, lanes] = optical_depth / (1.0 + jnp.exp(-x))
            return 0

        return lax.fori_loop(0, slices // UNROLL, slope_step, 0)

    lax.fori_loop(0, blocks, slope_block, 0)
    target_copy.wait()

    others = pl.ds(0, (slabs - 1) * message)
    pltpu.make_async_copy(partial_got.at[others], partial_got.at[others], recv_sem.at[0]).wait()

    codes[...] = as_floats(partial_got[...])

    def gathered(c):
        coded = jnp.concatenate(
            [
                codes[pl.ds(c * BAND_ROWS + j, slabs, stride=message), :]
                for j in range(BAND_ROWS)
            ],
            axis=1,
        )
        return from_log_code(coded, *codings[c])

    def mixed(matrix, value):
        return jnp.dot(
            matrix,
            value,
            precision=lax.Precision.HIGHEST,
            preferred_element_type=jnp.float32,
        )

    blocked = gathered(3)
    kept = 1.0 - blocked
    front = jnp.exp(mixed(earlier, jnp.log(kept)))
    arriving = front * blocked
    glow = jnp.zeros_like(front)
    expected = jnp.zeros_like(front)
    answers = []
    for c in range(3):
        mean = gathered(c)
        weighted = arriving * mean
        goal = jnp.concatenate(
            [target_in[c, pl.ds(my_band * BAND_ROWS + j, 1), :] for j in range(BAND_ROWS)], axis=1
        )
        residual = jnp.sum(weighted, axis=0, keepdims=True) - goal
        seen = front * residual
        glow = glow + residual * weighted
        expected = expected + seen * mean
        answers.append(seen)
    answers.append(mixed(later, glow) / kept - expected)
    scales = answer_scales()
    for c, value in enumerate(answers):
        coded = to_answer_code(value, scales[c])
        for j in range(BAND_ROWS):
            codes[pl.ds(c * BAND_ROWS + j, slabs, stride=message), :] = coded[
                :, j * LANES : (j + 1) * LANES
            ]
    answer_sent[...] = as_words(codes[...])

    def answer_copy(slab):
        return remote(
            answer_sent.at[rows_of(slab)],
            answer_got.at[rows_of(depth_at)],
            send_sem.at[1],
            recv_sem.at[1],
            "depth",
            slab,
        )

    def answer_start(k, _):
        block = block_at(k)
        for g in range(bands):
            slab = owner_at(block, g)

            @pl.when(slab != depth_at)
            def _():
                answer_copy(slab).start()

        return 0

    lax.fori_loop(0, blocks, answer_start, 0)
    answer_got[rows_of(depth_at), :] = answer_sent[rows_of(depth_at), :]

    for copy in (slice_up, slice_down, row_up, row_down):
        copy.wait()

    @pl.when(depth_at == 0)
    def _():
        dens[0] = dens[1]

    @pl.when(depth_at == slabs - 1)
    def _():
        dens[slices + 1] = dens[slices]

    rim[...] = rim_got[...].astype(jnp.float32)

    @pl.when(rows_at == 0)
    def _():
        rim[0] = edge[0]

    @pl.when(rows_at == groups - 1)
    def _():
        rim[1] = edge[1]

    def smooth_block(block, _):
        lanes = lanes_of(block)
        row = lax.broadcasted_iota(jnp.int32, (rows, LANES), 0)

        def smooth_step(step, carry):
            low, centre = carry
            chunk = pl.ds(pl.multiple_of(step * UNROLL, UNROLL), UNROLL)
            above, below = (rim[0, chunk, lanes], rim[1, chunk, lanes])
            for u in range(UNROLL):
                z = step * UNROLL + u
                high = dens[z + 2, :, lanes].astype(jnp.float32)
                upper = jnp.where(row == 0, above[u : u + 1], pltpu.roll(centre, 1, axis=0))
                lower = jnp.where(
                    row == rows - 1, below[u : u + 1], pltpu.roll(centre, rows - 1, axis=0)
                )
                smooth_out[z, :, lanes] = (2.0 * smooth_weight) * (
                    (centre - low) + (centre - high) + (centre - upper) + (centre - lower)
                )
                low, centre = centre, high
            return low, centre

        start = (dens[0, :, lanes].astype(jnp.float32), dens[1, :, lanes].astype(jnp.float32))
        lax.fori_loop(0, slices // UNROLL, smooth_step, start)
        return 0

    lax.fori_loop(0, blocks, smooth_block, 0)

    pltpu.make_async_copy(answer_got.at[others], answer_got.at[others], recv_sem.at[1]).wait()
    answer_out[...] = answer_got[...]
    pltpu.make_async_copy(partial_sent.at[others], partial_sent.at[others], send_sem.at[0]).wait()
    pltpu.make_async_copy(answer_sent.at[others], answer_sent.at[others], send_sem.at[1]).wait()


def gradient_kernel(
    slices_total,
    colour_ref,
    lit_ref,
    through_ref,
    slope_ref,
    smooth_ref,
    mean_ref,
    answer_ref,
    dens_grad_hbm,
    colour_grad_hbm,
    dens_grad,
    colour_grad,
    dens_sem,
    colour_sem,
):
    slices, rows, width = lit_ref.shape
    blocks = width // LANES
    bands = rows // BAND_ROWS
    message = 4 * BAND_ROWS
    band_rows = blocks * message
    scales = answer_scales()

    def output_copies(block):
        lanes = pl.ds(pl.multiple_of(block * LANES, LANES), LANES)
        return (
            pltpu.make_async_copy(
                dens_grad.at[:, :, lanes], dens_grad_hbm.at[:, :, lanes], dens_sem.at[block]
            ),
            pltpu.make_async_copy(
                colour_grad.at[:, :, :, lanes],
                colour_grad_hbm.at[:, :, :, lanes],
                colour_sem.at[block],
            ),
        )

    def gradient_block(block, _):
        lanes = pl.ds(pl.multiple_of(block * LANES, LANES), LANES)
        words = [
            as_floats(answer_ref[pl.ds(pl.multiple_of(g * band_rows + block * message, message), message), :])
            for g in range(bands)
        ]

        def answer(c):
            coded = [value[c * BAND_ROWS : (c + 1) * BAND_ROWS] for value in words]
            return from_answer_code(jnp.concatenate(coded, axis=0), scales[c])

        residual = [answer(c) for c in range(3)]
        whole = mean_ref[3, :, lanes] * answer(3)
        for c in range(3):
            whole = whole + residual[c] * mean_ref[c, :, lanes]
        strong = [slices_total * value for value in residual]

        def gradient_step(step, remaining):
            for u in range(UNROLL):
                z = step * UNROLL + u
                lit = lit_ref[z, :, lanes]
                seen = jnp.zeros_like(lit)
                for c in range(3):
                    colour = colour_ref[c, z, :, lanes]
                    seen = seen + residual[c] * colour
                    colour_grad[c, z, :, lanes] = (strong[c] * lit) * (colour * (1.0 - colour))
                remaining = remaining - lit * seen
                dens_grad[z, :, lanes] = (
                    slope_ref[z, :, lanes] * (through_ref[z, :, lanes] * seen - remaining)
                    + smooth_ref[z, :, lanes]
                )
            return remaining

        lax.fori_loop(0, slices // UNROLL, gradient_step, whole)
        for copy in output_copies(block):
            copy.start()
        return 0

    lax.fori_loop(0, blocks, gradient_block, 0)

    def finish(block, _):
        for copy in output_copies(block):
            copy.wait()
        return 0

    lax.fori_loop(0, blocks, finish, 0)


def local(slabs, groups, density_raw, colour_raw, target, slab_rank):
    slices, rows, width = density_raw.shape
    blocks = width // LANES
    message = 4 * BAND_ROWS
    voxels = (slices, rows, width)
    f32 = jnp.float32
    bf16 = jnp.bfloat16
    anywhere = pl.BlockSpec(memory_space=pl.ANY)
    vmem = pl.BlockSpec(memory_space=pltpu.VMEM)
    packet = pltpu.VMEM((slabs * message, LANES), jnp.int16)
    saved = pl.pallas_call(
        functools.partial(light_kernel, slabs, groups),
        out_shape=(
            pltpu.VMEM((3, *voxels), f32),
            pltpu.VMEM(voxels, f32),
            pltpu.VMEM(voxels, f32),
            pltpu.VMEM(voxels, f32),
            pltpu.VMEM(voxels, f32),
            pltpu.VMEM((4, rows, width), f32),
            packet,
        ),
        in_specs=[anywhere, anywhere, anywhere, pl.BlockSpec(memory_space=pltpu.SMEM)],
        out_specs=(vmem,) * 7,
        scratch_shapes=[
            pltpu.VMEM((slices + 2, rows, width), bf16),
            pltpu.VMEM((3, *voxels), bf16),
            pltpu.VMEM((3, rows, LANES), f32),
            pltpu.VMEM((2, slices, width), f32),
            pltpu.VMEM((2, slices, width), bf16),
            pltpu.VMEM((2, slices, width), bf16),
            pltpu.VMEM((2, slices, width), f32),
            packet,
            packet,
            packet,
            packet,
            pltpu.VMEM((slabs * message, LANES), f32),
            pltpu.SemaphoreType.DMA((blocks,)),
            pltpu.SemaphoreType.DMA((blocks,)),
            pltpu.SemaphoreType.DMA,
            pltpu.SemaphoreType.DMA((2,)),
            pltpu.SemaphoreType.DMA((2,)),
            pltpu.SemaphoreType.DMA((4,)),
            pltpu.SemaphoreType.DMA((4,)),
        ],
        compiler_params=pltpu.CompilerParams(
            collective_id=0, has_side_effects=True, vmem_limit_bytes=40 * 2**20
        ),
        name="light",
    )(density_raw, colour_raw, target, slab_rank)
    return pl.pallas_call(
        functools.partial(gradient_kernel, float(slices * slabs)),
        out_shape=(
            jax.ShapeDtypeStruct(voxels, f32),
            jax.ShapeDtypeStruct((3, *voxels), f32),
        ),
        in_specs=[vmem] * 7,
        out_specs=(anywhere, anywhere),
        scratch_shapes=[
            pltpu.VMEM(voxels, f32),
            pltpu.VMEM((3, *voxels), f32),
            pltpu.SemaphoreType.DMA((blocks,)),
            pltpu.SemaphoreType.DMA((blocks,)),
        ],
        compiler_params=pltpu.CompilerParams(vmem_limit_bytes=16 * 2**20),
        name="gradient",
    )(*saved)


def solution(mesh):
    return jax.shard_map(
        functools.partial(local, mesh.shape["depth"], mesh.shape["rows"]),
        mesh=mesh,
        in_specs=(P("depth", "rows", None), P(None, "depth", "rows", None), P(None, "rows", None), P()),
        out_specs=(P("depth", "rows", None), P(None, "depth", "rows", None)),
        check_vma=False,
    )
```

```python
import functools
import math

import jax
import jax.numpy as jnp
from jax import lax
from jax.experimental import pallas as pl
from jax.experimental.pallas import tpu as pltpu
from jax.sharding import PartitionSpec as P

optical_depth = 2.5
smooth_weight = 0.05

LANES = 128
BAND_ROWS = 4
UNROLL = 8
RAW_LIMIT = 6.0
CODE_TOP = 32767.0
ANSWER_KNEE = 2.0**-10


def log_code(least, most):
    low, high = (math.log(least) - 1e-3, math.log(most) + 1e-3)
    return (0.5 * (low + high), 2.0 * CODE_TOP / (high - low))


def partial_codes(slices, slices_total):
    soft = (math.log1p(math.exp(-RAW_LIMIT)), math.log1p(math.exp(RAW_LIMIT)))
    span = optical_depth / slices_total * slices
    blocked = [-math.expm1(-span * value) for value in soft]
    colour = [1.0 / (1.0 + math.exp(sign * RAW_LIMIT)) for sign in (1, -1)]
    return [log_code(*colour)] * 3 + [log_code(*blocked)]


def answer_scales():
    return [math.asinh(top / ANSWER_KNEE) / CODE_TOP for top in (1.001, 1.001, 1.001, 3.01)]


def to_code(value):
    kept = jnp.clip(value, -CODE_TOP, CODE_TOP)
    return jnp.floor(kept + 0.5)


def from_log_code(code, middle, scale):
    return jnp.exp(code * (1.0 / scale) + middle)


def to_answer_code(value, scale):
    tall = jnp.abs(value) * (1.0 / ANSWER_KNEE)
    code = jnp.log(tall + jnp.sqrt(tall * tall + 1.0)) * (1.0 / scale)
    return to_code(jnp.where(value < 0.0, -code, code))


def from_answer_code(code, scale):
    grown = jnp.exp(code * scale)
    return (0.5 * ANSWER_KNEE) * (grown - 1.0 / grown)


def far_first(k, count):
    return lax.rem(count // 2 + (2 * (k % 2) - 1) * ((k + 1) // 2) + count, count)


def as_words(code):
    return code.astype(jnp.int32).astype(jnp.int16)


def as_floats(words):
    return words.astype(jnp.int32).astype(jnp.float32)


def remote(src, dst, send_sem, recv_sem, axis, peer):
    return pltpu.make_async_remote_copy(
        src_ref=src,
        dst_ref=dst,
        send_sem=send_sem,
        recv_sem=recv_sem,
        device_id={axis: peer},
        device_id_type=pl.DeviceIdType.MESH,
    )


def light_kernel(
    slabs,
    groups,
    dens_hbm,
    colour_hbm,
    target_hbm,
    rank_hbm,
    colour_out,
    lit_out,
    through_out,
    slope_out,
    smooth_out,
    mean_out,
    answer_out,
    dens,
    colour_in,
    target_in,
    edge,
    edge_sent,
    rim_got,
    rim,
    partial_sent,
    partial_got,
    answer_sent,
    answer_got,
    codes,
    slice_got,
    rank_ref,
    rank_sem,
    dens_sem,
    colour_sem,
    target_sem,
    send_sem,
    recv_sem,
    rim_send_sem,
    rim_recv_sem,
):
    depth_at = lax.axis_index("depth")
    rows_at = lax.axis_index("rows")
    slices, rows, width = dens_hbm.shape
    blocks = width // LANES
    bands = rows // BAND_ROWS
    message = 4 * BAND_ROWS
    slices_total = slices * slabs
    step_depth = optical_depth / slices_total
    my_block = lax.rem(depth_at, blocks)
    my_band = depth_at // blocks
    codings = partial_codes(slices, slices_total)

    def lanes_of(block):
        return pl.ds(pl.multiple_of(block * LANES, LANES), LANES)

    def rows_of(slab):
        return pl.ds(pl.multiple_of(slab * message, message), message)

    def input_copies(block):
        lanes = lanes_of(block)
        return (
            pltpu.make_async_copy(
                dens_hbm.at[:, :, lanes], dens.at[block, pl.ds(1, slices)], dens_sem.at[block]
            ),
            pltpu.make_async_copy(
                colour_hbm.at[:, :, :, lanes], colour_in.at[block], colour_sem.at[block]
            ),
        )

    def block_at(k):
        return lax.rem(my_block + far_first(k, blocks), blocks)

    def owner_at(block, g):
        return lax.rem(my_band + far_first(g, bands), bands) * blocks + block

    barrier = pltpu.get_barrier_semaphore()

    def greet(k, _):
        block = block_at(k)
        for g in range(bands):
            peer = owner_at(block, g)

            @pl.when(peer != depth_at)
            def _():
                pl.semaphore_signal(
                    barrier,
                    inc=1,
                    device_id={"depth": peer},
                    device_id_type=pl.DeviceIdType.MESH,
                )

        return 0

    lax.fori_loop(0, blocks, greet, 0)
    rows_up = lax.rem(rows_at + 1, groups)
    rows_down = lax.rem(rows_at + groups - 1, groups)
    depth_up = lax.rem(depth_at + 1, slabs)
    depth_down = lax.rem(depth_at + slabs - 1, slabs)
    for peer in (rows_up, rows_down):
        pl.semaphore_signal(
            barrier, inc=1, device_id={"rows": peer}, device_id_type=pl.DeviceIdType.MESH
        )

    def start_inputs(k, _):
        for copy in input_copies(block_at(k)):
            copy.start()
        return 0

    lax.fori_loop(0, blocks, start_inputs, 0)
    target_copy = pltpu.make_async_copy(
        target_hbm.at[:, :, lanes_of(my_block)], target_in, target_sem
    )
    target_copy.start()
    rank_copy = pltpu.make_async_copy(rank_hbm, rank_ref, rank_sem)
    rank_copy.start()

    slice_up = remote(
        dens_hbm.at[slices - 1], slice_got.at[0], rim_send_sem.at[0], rim_recv_sem.at[0], "depth", depth_up
    )
    slice_down = remote(
        dens_hbm.at[0],
        slice_got.at[1],
        rim_send_sem.at[1],
        rim_recv_sem.at[1],
        "depth",
        depth_down,
    )
    row_up = remote(
        edge_sent.at[1], rim_got.at[0], rim_send_sem.at[2], rim_recv_sem.at[2], "rows", rows_up
    )
    row_down = remote(
        edge_sent.at[0], rim_got.at[1], rim_send_sem.at[3], rim_recv_sem.at[3], "rows", rows_down
    )

    def partial_copy(owner):
        return remote(
            partial_sent.at[rows_of(owner)],
            partial_got.at[rows_of(depth_at)],
            send_sem.at[0],
            recv_sem.at[0],
            "depth",
            owner,
        )

    def send_block(k, _):
        block = block_at(k)
        for g in range(bands):
            owner = owner_at(block, g)

            @pl.when(owner != depth_at)
            def _():
                partial_copy(owner).start()

        return 0

    send_from = jnp.where(my_block < blocks // 2, blocks - 1, 0)

    def forward_block(k, _):
        block = block_at(k)
        lanes = lanes_of(block)
        for copy in input_copies(block):
            copy.wait()

        def forward_step(step, carry):
            blocked, light, *shine = carry
            firsts, lasts = ([], [])
            for u in range(UNROLL):
                z = step * UNROLL + u
                x = dens[block, z + 1].astype(jnp.float32)
                firsts.append(x[:1])
                lasts.append(x[rows - 1 :])
                d = step_depth * jnp.log(1.0 + jnp.exp(x))
                opacity = d * (1.0 - d * (0.5 - d * (1.0 / 6.0 - d * (1.0 / 24.0))))
                lit = light * opacity
                blocked = blocked + lit
                light = light - lit
                lit_out[block, z] = lit
                through_out[block, z] = light
                for c in range(3):
                    raw = colour_in[block, c, z].astype(jnp.float32)
                    colour = 1.0 / (1.0 + jnp.exp(-raw))
                    colour_out[block, c, z] = colour
                    shine[c] = shine[c] + lit * colour
            chunk = pl.ds(pl.multiple_of(step * UNROLL, UNROLL), UNROLL)
            edge[0, chunk, lanes] = jnp.concatenate(firsts, axis=0)
            edge[1, chunk, lanes] = jnp.concatenate(lasts, axis=0)
            return (blocked, light, *shine)

        zero = jnp.zeros((rows, LANES), jnp.float32)
        blocked, light, *shine = lax.fori_loop(
            0, slices // UNROLL, forward_step, (zero, zero + 1.0, zero, zero, zero)
        )
        mean = [value / blocked for value in shine]
        for c in range(3):
            mean_out[block, c] = shine[c] + light * mean[c]
        mean_out[block, 3] = light
        coded = [
            to_code((jnp.log(value) - middle) * scale)
            for value, (middle, scale) in zip((*mean, blocked), codings)
        ]
        for g in range(bands):
            packed = [value[g * BAND_ROWS : (g + 1) * BAND_ROWS] for value in coded]
            partial_sent[rows_of(g * blocks + block), :] = as_words(
                jnp.concatenate(packed, axis=0)
            )

        @pl.when(k == send_from)
        def _():
            pl.semaphore_wait(barrier, slabs + 1)
            lax.fori_loop(0, k, send_block, 0)
            slice_up.start()
            slice_down.start()

        @pl.when(k >= send_from)
        def _():
            send_block(k, 0)

        return 0

    lax.fori_loop(0, blocks, forward_block, 0)
    partial_got[rows_of(depth_at), :] = partial_sent[rows_of(depth_at), :]
    edge_sent[...] = edge[...].astype(jnp.bfloat16)
    row_up.start()
    row_down.start()

    ranks_row = jnp.zeros((slabs, LANES), jnp.int32)
    ranks_column = jnp.zeros((slabs, LANES), jnp.int32)
    lane = lax.broadcasted_iota(jnp.int32, (slabs, LANES), 1)
    sub = lax.broadcasted_iota(jnp.int32, (slabs, LANES), 0)
    rank_copy.wait()
    for s in range(slabs):
        rank = rank_ref[s]
        ranks_row = jnp.where(lane % slabs == s, rank, ranks_row)
        ranks_column = jnp.where(sub == s, rank, ranks_column)
    thrice = 3 * slabs
    earlier = (ranks_row < ranks_column).astype(jnp.bfloat16)[:, :thrice]
    later = (ranks_row > ranks_column).astype(jnp.bfloat16)[:, :thrice]

    def slope_block(block, _):

        def slope_step(step, _):
            for u in range(UNROLL):
                z = step * UNROLL + u
                x = dens[block, z + 1].astype(jnp.float32)
                slope_out[block, z] = optical_depth / (1.0 + jnp.exp(-x))
            return 0

        return lax.fori_loop(0, slices // UNROLL, slope_step, 0)

    lax.fori_loop(0, blocks, slope_block, 0)
    target_copy.wait()

    others = pl.ds(0, (slabs - 1) * message)
    pltpu.make_async_copy(partial_got.at[others], partial_got.at[others], recv_sem.at[0]).wait()

    codes[...] = as_floats(partial_got[...])

    def gathered(c):
        coded = jnp.concatenate(
            [
                codes[pl.ds(c * BAND_ROWS + j, slabs, stride=message), :]
                for j in range(BAND_ROWS)
            ],
            axis=1,
        )
        return from_log_code(coded, *codings[c])

    def mixed(matrix, value):
        parts = []
        for _ in range(3):
            part = value.astype(jnp.bfloat16)
            value = value - part.astype(jnp.float32)
            parts.append(part)
        return jnp.dot(
            matrix, jnp.concatenate(parts, axis=0), preferred_element_type=jnp.float32
        )

    blocked = gathered(3)
    kept = 1.0 - blocked
    front = jnp.exp(mixed(earlier, jnp.log(kept)))
    arriving = front * blocked
    glow = jnp.zeros_like(front)
    expected = jnp.zeros_like(front)
    answers = []
    for c in range(3):
        mean = gathered(c)
        weighted = arriving * mean
        goal = jnp.concatenate(
            [target_in[c, pl.ds(my_band * BAND_ROWS + j, 1), :] for j in range(BAND_ROWS)], axis=1
        )
        residual = jnp.sum(weighted, axis=0, keepdims=True) - goal
        seen = front * residual
        glow = glow + residual * weighted
        expected = expected + seen * mean
        answers.append(seen)
    answers.append(mixed(later, glow) / kept - expected)
    scales = answer_scales()
    for c, value in enumerate(answers):
        coded = to_answer_code(value, scales[c])
        for j in range(BAND_ROWS):
            codes[pl.ds(c * BAND_ROWS + j, slabs, stride=message), :] = coded[
                :, j * LANES : (j + 1) * LANES
            ]
    answer_sent[...] = as_words(codes[...])

    def answer_copy(slab):
        return remote(
            answer_sent.at[rows_of(slab)],
            answer_got.at[rows_of(depth_at)],
            send_sem.at[1],
            recv_sem.at[1],
            "depth",
            slab,
        )

    def answer_start(k, _):
        block = block_at(k)
        for g in range(bands):
            slab = owner_at(block, g)

            @pl.when(slab != depth_at)
            def _():
                answer_copy(slab).start()

        return 0

    lax.fori_loop(0, blocks, answer_start, 0)
    answer_got[rows_of(depth_at), :] = answer_sent[rows_of(depth_at), :]

    for copy in (slice_up, slice_down, row_up, row_down):
        copy.wait()

    rim[...] = rim_got[...].astype(jnp.float32)

    @pl.when(rows_at == 0)
    def _():
        rim[0] = edge[0]

    @pl.when(rows_at == groups - 1)
    def _():
        rim[1] = edge[1]

    def smooth_block(block, _):
        lanes = lanes_of(block)
        row = lax.broadcasted_iota(jnp.int32, (rows, LANES), 0)

        def smooth_step(step, carry):
            low, centre = carry
            chunk = pl.ds(pl.multiple_of(step * UNROLL, UNROLL), UNROLL)
            above, below = (rim[0, chunk, lanes], rim[1, chunk, lanes])
            for u in range(UNROLL):
                z = step * UNROLL + u
                high = dens[block, z + 2].astype(jnp.float32)
                upper = jnp.where(row == 0, above[u : u + 1], pltpu.roll(centre, 1, axis=0))
                lower = jnp.where(
                    row == rows - 1, below[u : u + 1], pltpu.roll(centre, rows - 1, axis=0)
                )
                smooth_out[block, z] = (2.0 * smooth_weight) * (
                    (centre - low) + (centre - high) + (centre - upper) + (centre - lower)
                )
                low, centre = centre, high
            return low, centre

        first, last = (dens[block, 1], dens[block, slices])
        dens[block, 0] = jnp.where(depth_at == 0, first, slice_got[0, :, lanes])
        dens[block, slices + 1] = jnp.where(depth_at == slabs - 1, last, slice_got[1, :, lanes])
        start = (dens[block, 0].astype(jnp.float32), first.astype(jnp.float32))
        lax.fori_loop(0, slices // UNROLL, smooth_step, start)
        return 0

    lax.fori_loop(0, blocks, smooth_block, 0)

    pltpu.make_async_copy(answer_got.at[others], answer_got.at[others], recv_sem.at[1]).wait()
    answer_out[...] = answer_got[...]
    pltpu.make_async_copy(partial_sent.at[others], partial_sent.at[others], send_sem.at[0]).wait()
    pltpu.make_async_copy(answer_sent.at[others], answer_sent.at[others], send_sem.at[1]).wait()


def gradient_kernel(
    slices_total,
    colour_ref,
    lit_ref,
    through_ref,
    slope_ref,
    smooth_ref,
    mean_ref,
    answer_ref,
    dens_grad_hbm,
    colour_grad_hbm,
    dens_grad,
    colour_grad,
    dens_sem,
    colour_sem,
):
    blocks, slices, rows, _ = lit_ref.shape
    bands = rows // BAND_ROWS
    message = 4 * BAND_ROWS
    band_rows = blocks * message
    scales = answer_scales()

    def output_copies(block):
        lanes = pl.ds(pl.multiple_of(block * LANES, LANES), LANES)
        return (
            pltpu.make_async_copy(
                dens_grad.at[block], dens_grad_hbm.at[:, :, lanes], dens_sem.at[block]
            ),
            pltpu.make_async_copy(
                colour_grad.at[block],
                colour_grad_hbm.at[:, :, :, lanes],
                colour_sem.at[block],
            ),
        )

    def gradient_block(block, _):
        words = [
            as_floats(answer_ref[pl.ds(pl.multiple_of(g * band_rows + block * message, message), message), :])
            for g in range(bands)
        ]

        def answer(c):
            coded = [value[c * BAND_ROWS : (c + 1) * BAND_ROWS] for value in words]
            return from_answer_code(jnp.concatenate(coded, axis=0), scales[c])

        residual = [answer(c) for c in range(3)]
        whole = mean_ref[block, 3] * answer(3)
        for c in range(3):
            whole = whole + residual[c] * mean_ref[block, c]
        strong = [slices_total * value for value in residual]

        def gradient_step(step, remaining):
            for u in range(UNROLL):
                z = step * UNROLL + u
                lit = lit_ref[block, z]
                seen = jnp.zeros_like(lit)
                for c in range(3):
                    colour = colour_ref[block, c, z]
                    seen = seen + residual[c] * colour
                    colour_grad[block, c, z] = (strong[c] * lit) * (colour * (1.0 - colour))
                remaining = remaining - lit * seen
                dens_grad[block, z] = (
                    slope_ref[block, z] * (through_ref[block, z] * seen - remaining)
                    + smooth_ref[block, z]
                )
            return remaining

        lax.fori_loop(0, slices // UNROLL, gradient_step, whole)
        for copy in output_copies(block):
            copy.start()
        return 0

    lax.fori_loop(0, blocks, gradient_block, 0)

    def finish(block, _):
        for copy in output_copies(block):
            copy.wait()
        return 0

    lax.fori_loop(0, blocks, finish, 0)


def local(slabs, groups, density_raw, colour_raw, target, slab_rank):
    slices, rows, width = density_raw.shape
    blocks = width // LANES
    message = 4 * BAND_ROWS
    voxels = (slices, rows, width)
    blocked = (blocks, slices, rows, LANES)
    coloured = (blocks, 3, slices, rows, LANES)
    f32 = jnp.float32
    bf16 = jnp.bfloat16
    anywhere = pl.BlockSpec(memory_space=pl.ANY)
    vmem = pl.BlockSpec(memory_space=pltpu.VMEM)
    packet = pltpu.VMEM((slabs * message, LANES), jnp.int16)
    saved = pl.pallas_call(
        functools.partial(light_kernel, slabs, groups),
        out_shape=(
            pltpu.VMEM(coloured, f32),
            pltpu.VMEM(blocked, f32),
            pltpu.VMEM(blocked, f32),
            pltpu.VMEM(blocked, f32),
            pltpu.VMEM(blocked, f32),
            pltpu.VMEM((blocks, 4, rows, LANES), f32),
            packet,
        ),
        in_specs=[anywhere] * 4,
        out_specs=(vmem,) * 7,
        scratch_shapes=[
            pltpu.VMEM((blocks, slices + 2, rows, LANES), bf16),
            pltpu.VMEM(coloured, bf16),
            pltpu.VMEM((3, rows, LANES), f32),
            pltpu.VMEM((2, slices, width), f32),
            pltpu.VMEM((2, slices, width), bf16),
            pltpu.VMEM((2, slices, width), bf16),
            pltpu.VMEM((2, slices, width), f32),
            packet,
            packet,
            packet,
            packet,
            pltpu.VMEM((slabs * message, LANES), f32),
            pltpu.VMEM((2, rows, width), bf16),
            pltpu.SMEM((slabs,), jnp.int32),
            pltpu.SemaphoreType.DMA,
            pltpu.SemaphoreType.DMA((blocks,)),
            pltpu.SemaphoreType.DMA((blocks,)),
            pltpu.SemaphoreType.DMA,
            pltpu.SemaphoreType.DMA((2,)),
            pltpu.SemaphoreType.DMA((2,)),
            pltpu.SemaphoreType.DMA((4,)),
            pltpu.SemaphoreType.DMA((4,)),
        ],
        compiler_params=pltpu.CompilerParams(
            collective_id=0, has_side_effects=True, vmem_limit_bytes=40 * 2**20
        ),
        name="light",
    )(density_raw, colour_raw, target, slab_rank)
    return pl.pallas_call(
        functools.partial(gradient_kernel, float(slices * slabs)),
        out_shape=(
            jax.ShapeDtypeStruct(voxels, f32),
            jax.ShapeDtypeStruct((3, *voxels), f32),
        ),
        in_specs=[vmem] * 7,
        out_specs=(anywhere, anywhere),
        scratch_shapes=[
            pltpu.VMEM(blocked, f32),
            pltpu.VMEM(coloured, f32),
            pltpu.SemaphoreType.DMA((blocks,)),
            pltpu.SemaphoreType.DMA((blocks,)),
        ],
        compiler_params=pltpu.CompilerParams(vmem_limit_bytes=16 * 2**20),
        name="gradient",
    )(*saved)


def solution(mesh):
    return jax.shard_map(
        functools.partial(local, mesh.shape["depth"], mesh.shape["rows"]),
        mesh=mesh,
        in_specs=(P("depth", "rows", None), P(None, "depth", "rows", None), P(None, "rows", None), P()),
        out_specs=(P("depth", "rows", None), P(None, "depth", "rows", None)),
        check_vma=False,
    )
```

```python
import functools
import math

import jax
import jax.numpy as jnp
from jax import lax
from jax.experimental import pallas as pl
from jax.experimental.pallas import tpu as pltpu
from jax.sharding import PartitionSpec as P

optical_depth = 2.5
smooth_weight = 0.05

LANES = 128
BAND_ROWS = 4
UNROLL = 8
RAW_LIMIT = 6.0
CODE_TOP = 32767.0
ANSWER_KNEE = 2.0**-10


def log_code(least, most):
    low, high = (math.log(least) - 1e-3, math.log(most) + 1e-3)
    return (0.5 * (low + high), 2.0 * CODE_TOP / (high - low))


def partial_codes(slices, slices_total):
    soft = (math.log1p(math.exp(-RAW_LIMIT)), math.log1p(math.exp(RAW_LIMIT)))
    span = optical_depth / slices_total * slices
    blocked = [-math.expm1(-span * value) for value in soft]
    colour = [1.0 / (1.0 + math.exp(sign * RAW_LIMIT)) for sign in (1, -1)]
    return [log_code(*colour)] * 3 + [log_code(*blocked)]


def answer_scales():
    return [math.asinh(top / ANSWER_KNEE) / CODE_TOP for top in (1.001, 1.001, 1.001, 3.01)]


def to_code(value):
    kept = jnp.clip(value, -CODE_TOP, CODE_TOP)
    return jnp.floor(kept + 0.5)


def from_log_code(code, middle, scale):
    return jnp.exp(code * (1.0 / scale) + middle)


def to_answer_code(value, scale):
    tall = jnp.abs(value) * (1.0 / ANSWER_KNEE)
    code = jnp.log(tall + jnp.sqrt(tall * tall + 1.0)) * (1.0 / scale)
    return to_code(jnp.where(value < 0.0, -code, code))


def from_answer_code(code, scale):
    grown = jnp.exp(code * scale)
    return (0.5 * ANSWER_KNEE) * (grown - 1.0 / grown)


def far_first(k, count):
    return lax.rem(count // 2 + (2 * (k % 2) - 1) * ((k + 1) // 2) + count, count)


def as_words(code):
    return code.astype(jnp.int32).astype(jnp.int16)


def as_floats(words):
    return words.astype(jnp.int32).astype(jnp.float32)


def remote(src, dst, send_sem, recv_sem, axis, peer):
    return pltpu.make_async_remote_copy(
        src_ref=src,
        dst_ref=dst,
        send_sem=send_sem,
        recv_sem=recv_sem,
        device_id={axis: peer},
        device_id_type=pl.DeviceIdType.MESH,
    )


def light_kernel(
    slabs,
    groups,
    dens_hbm,
    colour_hbm,
    target_hbm,
    rank_hbm,
    colour_out,
    lit_out,
    through_out,
    slope_out,
    smooth_out,
    mean_out,
    answer_out,
    dens,
    colour_in,
    target_in,
    edge,
    edge_sent,
    rim_got,
    rim,
    partial_sent,
    partial_got,
    answer_sent,
    answer_got,
    codes,
    slice_got,
    rank_ref,
    rank_sem,
    dens_sem,
    colour_sem,
    target_sem,
    send_sem,
    recv_sem,
    rim_send_sem,
    rim_recv_sem,
):
    depth_at = lax.axis_index("depth")
    rows_at = lax.axis_index("rows")
    slices, rows, width = dens_hbm.shape
    blocks = width // LANES
    bands = rows // BAND_ROWS
    message = 4 * BAND_ROWS
    slices_total = slices * slabs
    step_depth = optical_depth / slices_total
    my_block = lax.rem(depth_at, blocks)
    my_band = depth_at // blocks
    codings = partial_codes(slices, slices_total)

    def lanes_of(block):
        return pl.ds(pl.multiple_of(block * LANES, LANES), LANES)

    def rows_of(slab):
        return pl.ds(pl.multiple_of(slab * message, message), message)

    def input_copies(block):
        lanes = lanes_of(block)
        return (
            pltpu.make_async_copy(
                dens_hbm.at[:, :, lanes], dens.at[block, pl.ds(1, slices)], dens_sem.at[block]
            ),
            pltpu.make_async_copy(
                colour_hbm.at[:, :, :, lanes], colour_in.at[block], colour_sem.at[block]
            ),
        )

    def block_at(k):
        return lax.rem(my_block + far_first(k, blocks), blocks)

    def owner_at(block, g):
        return lax.rem(my_band + far_first(g, bands), bands) * blocks + block

    barrier = pltpu.get_barrier_semaphore()

    def greet(k, _):
        block = block_at(k)
        for g in range(bands):
            peer = owner_at(block, g)

            @pl.when(peer != depth_at)
            def _():
                pl.semaphore_signal(
                    barrier,
                    inc=1,
                    device_id={"depth": peer},
                    device_id_type=pl.DeviceIdType.MESH,
                )

        return 0

    lax.fori_loop(0, blocks, greet, 0)
    rows_up = lax.rem(rows_at + 1, groups)
    rows_down = lax.rem(rows_at + groups - 1, groups)
    depth_up = lax.rem(depth_at + 1, slabs)
    depth_down = lax.rem(depth_at + slabs - 1, slabs)
    for peer in (rows_up, rows_down):
        pl.semaphore_signal(
            barrier, inc=1, device_id={"rows": peer}, device_id_type=pl.DeviceIdType.MESH
        )

    def start_inputs(k, _):
        for copy in input_copies(block_at(k)):
            copy.start()
        return 0

    lax.fori_loop(0, blocks, start_inputs, 0)
    target_copy = pltpu.make_async_copy(
        target_hbm.at[:, :, lanes_of(my_block)], target_in, target_sem
    )
    target_copy.start()
    rank_copy = pltpu.make_async_copy(rank_hbm, rank_ref, rank_sem)
    rank_copy.start()

    slice_up = remote(
        dens_hbm.at[slices - 1], slice_got.at[0], rim_send_sem.at[0], rim_recv_sem.at[0], "depth", depth_up
    )
    slice_down = remote(
        dens_hbm.at[0],
        slice_got.at[1],
        rim_send_sem.at[1],
        rim_recv_sem.at[1],
        "depth",
        depth_down,
    )
    row_up = remote(
        edge_sent.at[1], rim_got.at[0], rim_send_sem.at[2], rim_recv_sem.at[2], "rows", rows_up
    )
    row_down = remote(
        edge_sent.at[0], rim_got.at[1], rim_send_sem.at[3], rim_recv_sem.at[3], "rows", rows_down
    )

    def partial_copy(owner):
        return remote(
            partial_sent.at[rows_of(owner)],
            partial_got.at[rows_of(depth_at)],
            send_sem.at[0],
            recv_sem.at[0],
            "depth",
            owner,
        )

    def send_block(k, _):
        block = block_at(k)
        for g in range(bands):
            owner = owner_at(block, g)

            @pl.when(owner != depth_at)
            def _():
                partial_copy(owner).start()

        return 0

    send_from = jnp.where(my_block < blocks // 2, blocks - 1, 0)

    def forward_block(k, _):
        block = block_at(k)
        lanes = lanes_of(block)
        for copy in input_copies(block):
            copy.wait()

        def forward_step(step, carry):
            blocked, light, *shine = carry
            firsts, lasts = ([], [])
            for u in range(UNROLL):
                z = step * UNROLL + u
                x = dens[block, z + 1].astype(jnp.float32)
                firsts.append(x[:1])
                lasts.append(x[rows - 1 :])
                d = step_depth * jnp.log(1.0 + jnp.exp(x))
                opacity = d * (1.0 - d * (0.5 - d * (1.0 / 6.0 - d * (1.0 / 24.0))))
                lit = light * opacity
                blocked = blocked + lit
                light = light - lit
                lit_out[block, z] = lit
                through_out[block, z] = light
                for c in range(3):
                    raw = colour_in[block, c, z].astype(jnp.float32)
                    colour = 1.0 / (1.0 + jnp.exp(-raw))
                    colour_out[block, c, z] = colour
                    shine[c] = shine[c] + lit * colour
            chunk = pl.ds(pl.multiple_of(step * UNROLL, UNROLL), UNROLL)
            edge[0, chunk, lanes] = jnp.concatenate(firsts, axis=0)
            edge[1, chunk, lanes] = jnp.concatenate(lasts, axis=0)
            return (blocked, light, *shine)

        zero = jnp.zeros((rows, LANES), jnp.float32)
        blocked, light, *shine = lax.fori_loop(
            0, slices // UNROLL, forward_step, (zero, zero + 1.0, zero, zero, zero)
        )
        mean = [value / blocked for value in shine]
        for c in range(3):
            mean_out[block, c] = shine[c] + light * mean[c]
        mean_out[block, 3] = light
        coded = [
            to_code((jnp.log(value) - middle) * scale)
            for value, (middle, scale) in zip((*mean, blocked), codings)
        ]
        for g in range(bands):
            packed = [value[g * BAND_ROWS : (g + 1) * BAND_ROWS] for value in coded]
            partial_sent[rows_of(g * blocks + block), :] = as_words(
                jnp.concatenate(packed, axis=0)
            )

        @pl.when(k == send_from)
        def _():
            pl.semaphore_wait(barrier, slabs + 1)
            lax.fori_loop(0, k, send_block, 0)
            slice_up.start()
            slice_down.start()

        @pl.when(k >= send_from)
        def _():
            send_block(k, 0)

        return 0

    lax.fori_loop(0, blocks, forward_block, 0)
    partial_got[rows_of(depth_at), :] = partial_sent[rows_of(depth_at), :]
    edge_sent[...] = edge[...].astype(jnp.bfloat16)
    row_up.start()
    row_down.start()

    ranks_row = jnp.zeros((slabs, LANES), jnp.int32)
    ranks_column = jnp.zeros((slabs, LANES), jnp.int32)
    lane = lax.broadcasted_iota(jnp.int32, (slabs, LANES), 1)
    sub = lax.broadcasted_iota(jnp.int32, (slabs, LANES), 0)
    rank_copy.wait()
    for s in range(slabs):
        rank = rank_ref[s]
        ranks_row = jnp.where(lane % slabs == s, rank, ranks_row)
        ranks_column = jnp.where(sub == s, rank, ranks_column)
    thrice = 3 * slabs
    earlier = (ranks_row < ranks_column).astype(jnp.bfloat16)[:, :thrice]
    later = (ranks_row > ranks_column).astype(jnp.bfloat16)[:, :thrice]

    def slope_block(block, _):

        def slope_step(step, _):
            for u in range(UNROLL):
                z = step * UNROLL + u
                x = dens[block, z + 1].astype(jnp.float32)
                slope_out[block, z] = optical_depth / (1.0 + jnp.exp(-x))
            return 0

        return lax.fori_loop(0, slices // UNROLL, slope_step, 0)

    lax.fori_loop(0, blocks, slope_block, 0)
    target_copy.wait()

    others = pl.ds(0, (slabs - 1) * message)
    pltpu.make_async_copy(partial_got.at[others], partial_got.at[others], recv_sem.at[0]).wait()

    codes[...] = as_floats(partial_got[...])

    def gathered(c):
        coded = jnp.concatenate(
            [
                codes[pl.ds(c * BAND_ROWS + j, slabs, stride=message), :]
                for j in range(BAND_ROWS)
            ],
            axis=1,
        )
        return from_log_code(coded, *codings[c])

    def mixed(matrix, value):
        parts = []
        for _ in range(3):
            part = value.astype(jnp.bfloat16)
            value = value - part.astype(jnp.float32)
            parts.append(part)
        return jnp.dot(
            matrix, jnp.concatenate(parts, axis=0), preferred_element_type=jnp.float32
        )

    blocked = gathered(3)
    kept = 1.0 - blocked
    front = jnp.exp(mixed(earlier, jnp.log(kept)))
    arriving = front * blocked
    glow = jnp.zeros_like(front)
    expected = jnp.zeros_like(front)
    answers = []
    for c in range(3):
        mean = gathered(c)
        weighted = arriving * mean
        goal = jnp.concatenate(
            [target_in[c, pl.ds(my_band * BAND_ROWS + j, 1), :] for j in range(BAND_ROWS)], axis=1
        )
        residual = jnp.sum(weighted, axis=0, keepdims=True) - goal
        seen = front * residual
        glow = glow + residual * weighted
        expected = expected + seen * mean
        answers.append(seen)
    answers.append(mixed(later, glow) / kept - expected)
    scales = answer_scales()
    for c, value in enumerate(answers):
        coded = to_answer_code(value, scales[c])
        for j in range(BAND_ROWS):
            codes[pl.ds(c * BAND_ROWS + j, slabs, stride=message), :] = coded[
                :, j * LANES : (j + 1) * LANES
            ]
    answer_sent[...] = as_words(codes[...])

    def answer_copy(slab):
        return remote(
            answer_sent.at[rows_of(slab)],
            answer_got.at[rows_of(depth_at)],
            send_sem.at[1],
            recv_sem.at[1],
            "depth",
            slab,
        )

    def answer_start(k, _):
        block = block_at(k)
        for g in range(bands):
            slab = owner_at(block, g)

            @pl.when(slab != depth_at)
            def _():
                answer_copy(slab).start()

        return 0

    lax.fori_loop(0, blocks, answer_start, 0)
    answer_got[rows_of(depth_at), :] = answer_sent[rows_of(depth_at), :]

    for copy in (slice_up, slice_down, row_up, row_down):
        copy.wait()

    rim[...] = rim_got[...].astype(jnp.float32)

    @pl.when(rows_at == 0)
    def _():
        rim[0] = edge[0]

    @pl.when(rows_at == groups - 1)
    def _():
        rim[1] = edge[1]

    def smooth_block(block, _):
        lanes = lanes_of(block)
        row = lax.broadcasted_iota(jnp.int32, (rows, LANES), 0)

        def smooth_step(step, carry):
            low, centre = carry
            chunk = pl.ds(pl.multiple_of(step * UNROLL, UNROLL), UNROLL)
            above, below = (rim[0, chunk, lanes], rim[1, chunk, lanes])
            for u in range(UNROLL):
                z = step * UNROLL + u
                high = dens[block, z + 2].astype(jnp.float32)
                upper = jnp.where(row == 0, above[u : u + 1], pltpu.roll(centre, 1, axis=0))
                lower = jnp.where(
                    row == rows - 1, below[u : u + 1], pltpu.roll(centre, rows - 1, axis=0)
                )
                smooth_out[block, z] = (2.0 * smooth_weight) * (
                    (centre - low) + (centre - high) + (centre - upper) + (centre - lower)
                )
                low, centre = centre, high
            return low, centre

        first, last = (dens[block, 1], dens[block, slices])
        dens[block, 0] = jnp.where(depth_at == 0, first, slice_got[0, :, lanes])
        dens[block, slices + 1] = jnp.where(depth_at == slabs - 1, last, slice_got[1, :, lanes])
        start = (dens[block, 0].astype(jnp.float32), first.astype(jnp.float32))
        lax.fori_loop(0, slices // UNROLL, smooth_step, start)
        return 0

    lax.fori_loop(0, blocks, smooth_block, 0)

    pltpu.make_async_copy(partial_sent.at[others], partial_sent.at[others], send_sem.at[0]).wait()
    pltpu.make_async_copy(answer_sent.at[others], answer_sent.at[others], send_sem.at[1]).wait()
    pltpu.make_async_copy(answer_got.at[others], answer_got.at[others], recv_sem.at[1]).wait()
    answer_out[...] = answer_got[...]


def gradient_kernel(
    slices_total,
    colour_ref,
    lit_ref,
    through_ref,
    slope_ref,
    smooth_ref,
    mean_ref,
    answer_ref,
    dens_grad_hbm,
    colour_grad_hbm,
    dens_grad,
    colour_grad,
    dens_sem,
    colour_sem,
):
    blocks, slices, rows, _ = lit_ref.shape
    bands = rows // BAND_ROWS
    message = 4 * BAND_ROWS
    band_rows = blocks * message
    scales = answer_scales()

    def output_copies(block, start, count):
        some = pl.ds(start, count)
        lanes = pl.ds(pl.multiple_of(block * LANES, LANES), LANES)
        return (
            pltpu.make_async_copy(
                dens_grad.at[block, some], dens_grad_hbm.at[some, :, lanes], dens_sem.at[block]
            ),
            pltpu.make_async_copy(
                colour_grad.at[block, :, some],
                colour_grad_hbm.at[:, some, :, lanes],
                colour_sem.at[block],
            ),
        )

    def gradient_block(block, _):
        words = [
            as_floats(answer_ref[pl.ds(pl.multiple_of(g * band_rows + block * message, message), message), :])
            for g in range(bands)
        ]

        def answer(c):
            coded = [value[c * BAND_ROWS : (c + 1) * BAND_ROWS] for value in words]
            return from_answer_code(jnp.concatenate(coded, axis=0), scales[c])

        residual = [answer(c) for c in range(3)]
        whole = mean_ref[block, 3] * answer(3)
        for c in range(3):
            whole = whole + residual[c] * mean_ref[block, c]
        strong = [slices_total * value for value in residual]

        def gradient_step(step, remaining):
            for u in range(UNROLL):
                z = step * UNROLL + u
                lit = lit_ref[block, z]
                seen = jnp.zeros_like(lit)
                for c in range(3):
                    colour = colour_ref[block, c, z]
                    seen = seen + residual[c] * colour
                    colour_grad[block, c, z] = (strong[c] * lit) * (colour * (1.0 - colour))
                remaining = remaining - lit * seen
                dens_grad[block, z] = (
                    slope_ref[block, z] * (through_ref[block, z] * seen - remaining)
                    + smooth_ref[block, z]
                )
            for copy in output_copies(block, step * UNROLL, UNROLL):
                copy.start()
            return remaining

        lax.fori_loop(0, slices // UNROLL, gradient_step, whole)
        return 0

    lax.fori_loop(0, blocks, gradient_block, 0)

    def finish(block, _):
        for copy in output_copies(block, 0, slices):
            copy.wait()
        return 0

    lax.fori_loop(0, blocks, finish, 0)


def local(slabs, groups, density_raw, colour_raw, target, slab_rank):
    slices, rows, width = density_raw.shape
    blocks = width // LANES
    message = 4 * BAND_ROWS
    voxels = (slices, rows, width)
    blocked = (blocks, slices, rows, LANES)
    coloured = (blocks, 3, slices, rows, LANES)
    f32 = jnp.float32
    bf16 = jnp.bfloat16
    anywhere = pl.BlockSpec(memory_space=pl.ANY)
    vmem = pl.BlockSpec(memory_space=pltpu.VMEM)
    packet = pltpu.VMEM((slabs * message, LANES), jnp.int16)
    saved = pl.pallas_call(
        functools.partial(light_kernel, slabs, groups),
        out_shape=(
            pltpu.VMEM(coloured, f32),
            pltpu.VMEM(blocked, f32),
            pltpu.VMEM(blocked, f32),
            pltpu.VMEM(blocked, f32),
            pltpu.VMEM(blocked, f32),
            pltpu.VMEM((blocks, 4, rows, LANES), f32),
            packet,
        ),
        in_specs=[anywhere] * 4,
        out_specs=(vmem,) * 7,
        scratch_shapes=[
            pltpu.VMEM((blocks, slices + 2, rows, LANES), bf16),
            pltpu.VMEM(coloured, bf16),
            pltpu.VMEM((3, rows, LANES), f32),
            pltpu.VMEM((2, slices, width), f32),
            pltpu.VMEM((2, slices, width), bf16),
            pltpu.VMEM((2, slices, width), bf16),
            pltpu.VMEM((2, slices, width), f32),
            packet,
            packet,
            packet,
            packet,
            pltpu.VMEM((slabs * message, LANES), f32),
            pltpu.VMEM((2, rows, width), bf16),
            pltpu.SMEM((slabs,), jnp.int32),
            pltpu.SemaphoreType.DMA,
            pltpu.SemaphoreType.DMA((blocks,)),
            pltpu.SemaphoreType.DMA((blocks,)),
            pltpu.SemaphoreType.DMA,
            pltpu.SemaphoreType.DMA((2,)),
            pltpu.SemaphoreType.DMA((2,)),
            pltpu.SemaphoreType.DMA((4,)),
            pltpu.SemaphoreType.DMA((4,)),
        ],
        compiler_params=pltpu.CompilerParams(
            collective_id=0, has_side_effects=True, vmem_limit_bytes=40 * 2**20
        ),
        name="light",
    )(density_raw, colour_raw, target, slab_rank)
    return pl.pallas_call(
        functools.partial(gradient_kernel, float(slices * slabs)),
        out_shape=(
            jax.ShapeDtypeStruct(voxels, f32),
            jax.ShapeDtypeStruct((3, *voxels), f32),
        ),
        in_specs=[vmem] * 7,
        out_specs=(anywhere, anywhere),
        scratch_shapes=[
            pltpu.VMEM(blocked, f32),
            pltpu.VMEM(coloured, f32),
            pltpu.SemaphoreType.DMA((blocks,)),
            pltpu.SemaphoreType.DMA((blocks,)),
        ],
        compiler_params=pltpu.CompilerParams(vmem_limit_bytes=16 * 2**20),
        name="gradient",
    )(*saved)


def solution(mesh):
    return jax.shard_map(
        functools.partial(local, mesh.shape["depth"], mesh.shape["rows"]),
        mesh=mesh,
        in_specs=(P("depth", "rows", None), P(None, "depth", "rows", None), P(None, "rows", None), P()),
        out_specs=(P("depth", "rows", None), P(None, "depth", "rows", None)),
        check_vma=False,
    )
```

```python
import functools
import math

import jax
import jax.numpy as jnp
from jax import lax
from jax.experimental import pallas as pl
from jax.experimental.pallas import tpu as pltpu
from jax.sharding import PartitionSpec as P

optical_depth = 2.5
smooth_weight = 0.05

LANES = 128
BAND_ROWS = 4
UNROLL = 8
RAW_LIMIT = 6.0
CODE_TOP = 32767.0
ANSWER_KNEE = 2.0**-10


def log_code(least, most):
    low, high = (math.log(least) - 1e-3, math.log(most) + 1e-3)
    return (0.5 * (low + high), 2.0 * CODE_TOP / (high - low))


def partial_codes(slices, slices_total):
    soft = (math.log1p(math.exp(-RAW_LIMIT)), math.log1p(math.exp(RAW_LIMIT)))
    span = optical_depth / slices_total * slices
    blocked = [-math.expm1(-span * value) for value in soft]
    colour = [1.0 / (1.0 + math.exp(sign * RAW_LIMIT)) for sign in (1, -1)]
    return [log_code(*colour)] * 3 + [log_code(*blocked)]


def answer_scales():
    return [math.asinh(top / ANSWER_KNEE) / CODE_TOP for top in (1.001, 1.001, 1.001, 3.01)]


def to_code(value):
    kept = jnp.clip(value, -CODE_TOP, CODE_TOP)
    return jnp.floor(kept + 0.5)


def from_log_code(code, middle, scale):
    return jnp.exp(code * (1.0 / scale) + middle)


def to_answer_code(value, scale):
    tall = jnp.abs(value) * (1.0 / ANSWER_KNEE)
    code = jnp.log(tall + jnp.sqrt(tall * tall + 1.0)) * (1.0 / scale)
    return to_code(jnp.where(value < 0.0, -code, code))


def from_answer_code(code, scale):
    grown = jnp.exp(code * scale)
    return (0.5 * ANSWER_KNEE) * (grown - 1.0 / grown)


def far_first(k, count):
    return lax.rem(count // 2 + (2 * (k % 2) - 1) * ((k + 1) // 2) + count, count)


def as_words(code):
    return code.astype(jnp.int32).astype(jnp.int16)


def as_floats(words):
    return words.astype(jnp.int32).astype(jnp.float32)


def remote(src, dst, send_sem, recv_sem, axis, peer):
    return pltpu.make_async_remote_copy(
        src_ref=src,
        dst_ref=dst,
        send_sem=send_sem,
        recv_sem=recv_sem,
        device_id={axis: peer},
        device_id_type=pl.DeviceIdType.MESH,
    )


def light_kernel(
    slabs,
    groups,
    dens_hbm,
    colour_hbm,
    target_hbm,
    rank_hbm,
    colour_out,
    lit_out,
    through_out,
    slope_out,
    smooth_out,
    mean_out,
    answer_out,
    dens,
    colour_in,
    target_in,
    edge,
    edge_sent,
    rim_got,
    rim,
    partial_sent,
    partial_got,
    answer_sent,
    answer_got,
    codes,
    slice_got,
    rank_ref,
    rank_sem,
    dens_sem,
    colour_sem,
    target_sem,
    send_sem,
    recv_sem,
    rim_send_sem,
    rim_recv_sem,
):
    depth_at = lax.axis_index("depth")
    rows_at = lax.axis_index("rows")
    slices, rows, width = dens_hbm.shape
    blocks = width // LANES
    bands = rows // BAND_ROWS
    message = 4 * BAND_ROWS
    slices_total = slices * slabs
    step_depth = optical_depth / slices_total
    my_block = lax.rem(depth_at, blocks)
    my_band = depth_at // blocks
    codings = partial_codes(slices, slices_total)

    def lanes_of(block):
        return pl.ds(pl.multiple_of(block * LANES, LANES), LANES)

    def rows_of(slab):
        return pl.ds(pl.multiple_of(slab * message, message), message)

    def input_copies(block):
        lanes = lanes_of(block)
        return (
            pltpu.make_async_copy(
                dens_hbm.at[:, :, lanes], dens.at[block, pl.ds(1, slices)], dens_sem.at[block]
            ),
            pltpu.make_async_copy(
                colour_hbm.at[:, :, :, lanes], colour_in.at[block], colour_sem.at[block]
            ),
        )

    def block_at(k):
        return lax.rem(my_block + far_first(k, blocks), blocks)

    def owner_at(block, g):
        return lax.rem(my_band + far_first(g, bands), bands) * blocks + block

    barrier = pltpu.get_barrier_semaphore()

    def greet(k, _):
        block = block_at(k)
        for g in range(bands):
            peer = owner_at(block, g)

            @pl.when(peer != depth_at)
            def _():
                pl.semaphore_signal(
                    barrier,
                    inc=1,
                    device_id={"depth": peer},
                    device_id_type=pl.DeviceIdType.MESH,
                )

        return 0

    lax.fori_loop(0, blocks, greet, 0)
    rows_up = lax.rem(rows_at + 1, groups)
    rows_down = lax.rem(rows_at + groups - 1, groups)
    depth_up = lax.rem(depth_at + 1, slabs)
    depth_down = lax.rem(depth_at + slabs - 1, slabs)
    for peer in (rows_up, rows_down):
        pl.semaphore_signal(
            barrier, inc=1, device_id={"rows": peer}, device_id_type=pl.DeviceIdType.MESH
        )

    def start_inputs(k, _):
        for copy in input_copies(block_at(k)):
            copy.start()
        return 0

    lax.fori_loop(0, blocks, start_inputs, 0)
    target_copy = pltpu.make_async_copy(
        target_hbm.at[:, :, lanes_of(my_block)], target_in, target_sem
    )
    target_copy.start()
    rank_copy = pltpu.make_async_copy(rank_hbm, rank_ref, rank_sem)
    rank_copy.start()

    slice_up = remote(
        dens_hbm.at[slices - 1], slice_got.at[0], rim_send_sem.at[0], rim_recv_sem.at[0], "depth", depth_up
    )
    slice_down = remote(
        dens_hbm.at[0],
        slice_got.at[1],
        rim_send_sem.at[1],
        rim_recv_sem.at[1],
        "depth",
        depth_down,
    )
    row_up = remote(
        edge_sent.at[1], rim_got.at[0], rim_send_sem.at[2], rim_recv_sem.at[2], "rows", rows_up
    )
    row_down = remote(
        edge_sent.at[0], rim_got.at[1], rim_send_sem.at[3], rim_recv_sem.at[3], "rows", rows_down
    )

    def partial_copy(owner):
        return remote(
            partial_sent.at[rows_of(owner)],
            partial_got.at[rows_of(depth_at)],
            send_sem.at[0],
            recv_sem.at[0],
            "depth",
            owner,
        )

    def send_block(k, _):
        block = block_at(k)
        for g in range(bands):
            owner = owner_at(block, g)

            @pl.when(owner != depth_at)
            def _():
                partial_copy(owner).start()

        return 0

    send_from = jnp.where(my_block < blocks // 2, blocks - 1, 0)

    def forward_block(k, _):
        block = block_at(k)
        lanes = lanes_of(block)
        for copy in input_copies(block):
            copy.wait()

        def forward_step(step, carry):
            blocked, light, *shine = carry
            firsts, lasts = ([], [])
            for u in range(UNROLL):
                z = step * UNROLL + u
                x = dens[block, z + 1].astype(jnp.float32)
                firsts.append(x[:1])
                lasts.append(x[rows - 1 :])
                d = step_depth * jnp.log(1.0 + jnp.exp(x))
                opacity = d * (1.0 - d * (0.5 - d * (1.0 / 6.0 - d * (1.0 / 24.0))))
                lit = light * opacity
                blocked = blocked + lit
                light = light - lit
                lit_out[block, z] = lit
                through_out[block, z] = light
                for c in range(3):
                    raw = colour_in[block, c, z].astype(jnp.float32)
                    colour = 1.0 / (1.0 + jnp.exp(-raw))
                    colour_out[block, c, z] = colour
                    shine[c] = shine[c] + lit * colour
            chunk = pl.ds(pl.multiple_of(step * UNROLL, UNROLL), UNROLL)
            edge[0, chunk, lanes] = jnp.concatenate(firsts, axis=0)
            edge[1, chunk, lanes] = jnp.concatenate(lasts, axis=0)
            return (blocked, light, *shine)

        zero = jnp.zeros((rows, LANES), jnp.float32)
        blocked, light, *shine = lax.fori_loop(
            0, slices // UNROLL, forward_step, (zero, zero + 1.0, zero, zero, zero)
        )
        mean = [value / blocked for value in shine]
        for c in range(3):
            mean_out[block, c] = shine[c] + light * mean[c]
        mean_out[block, 3] = light
        coded = [
            to_code((jnp.log(value) - middle) * scale)
            for value, (middle, scale) in zip((*mean, blocked), codings)
        ]
        for g in range(bands):
            packed = [value[g * BAND_ROWS : (g + 1) * BAND_ROWS] for value in coded]
            partial_sent[rows_of(g * blocks + block), :] = as_words(
                jnp.concatenate(packed, axis=0)
            )

        @pl.when(k == send_from)
        def _():
            pl.semaphore_wait(barrier, slabs + 1)
            lax.fori_loop(0, k, send_block, 0)
            slice_up.start()
            slice_down.start()

        @pl.when(k >= send_from)
        def _():
            send_block(k, 0)

        return 0

    lax.fori_loop(0, blocks, forward_block, 0)
    partial_got[rows_of(depth_at), :] = partial_sent[rows_of(depth_at), :]
    edge_sent[...] = edge[...].astype(jnp.bfloat16)
    row_up.start()
    row_down.start()

    ranks_row = jnp.zeros((slabs, LANES), jnp.int32)
    ranks_column = jnp.zeros((slabs, LANES), jnp.int32)
    lane = lax.broadcasted_iota(jnp.int32, (slabs, LANES), 1)
    sub = lax.broadcasted_iota(jnp.int32, (slabs, LANES), 0)
    rank_copy.wait()
    for s in range(slabs):
        rank = rank_ref[s]
        ranks_row = jnp.where(lane % slabs == s, rank, ranks_row)
        ranks_column = jnp.where(sub == s, rank, ranks_column)
    thrice = 3 * slabs
    earlier = (ranks_row < ranks_column).astype(jnp.bfloat16)[:, :thrice]
    later = (ranks_row > ranks_column).astype(jnp.bfloat16)[:, :thrice]

    def slope_block(block, _):

        def slope_step(step, _):
            for u in range(UNROLL):
                z = step * UNROLL + u
                x = dens[block, z + 1].astype(jnp.float32)
                slope_out[block, z] = optical_depth / (1.0 + jnp.exp(-x))
            return 0

        return lax.fori_loop(0, slices // UNROLL, slope_step, 0)

    lax.fori_loop(0, blocks, slope_block, 0)
    target_copy.wait()

    others = pl.ds(0, (slabs - 1) * message)
    pltpu.make_async_copy(partial_got.at[others], partial_got.at[others], recv_sem.at[0]).wait()

    codes[...] = as_floats(partial_got[...])

    def gathered(c):
        coded = jnp.concatenate(
            [
                codes[pl.ds(c * BAND_ROWS + j, slabs, stride=message), :]
                for j in range(BAND_ROWS)
            ],
            axis=1,
        )
        return from_log_code(coded, *codings[c])

    def mixed(matrix, value):
        parts = []
        for _ in range(3):
            part = value.astype(jnp.bfloat16)
            value = value - part.astype(jnp.float32)
            parts.append(part)
        return jnp.dot(
            matrix, jnp.concatenate(parts, axis=0), preferred_element_type=jnp.float32
        )

    blocked = gathered(3)
    kept = 1.0 - blocked
    front = jnp.exp(mixed(earlier, jnp.log(kept)))
    arriving = front * blocked
    glow = jnp.zeros_like(front)
    expected = jnp.zeros_like(front)
    answers = []
    for c in range(3):
        mean = gathered(c)
        weighted = arriving * mean
        goal = jnp.concatenate(
            [target_in[c, pl.ds(my_band * BAND_ROWS + j, 1), :] for j in range(BAND_ROWS)], axis=1
        )
        residual = jnp.sum(weighted, axis=0, keepdims=True) - goal
        seen = front * residual
        glow = glow + residual * weighted
        expected = expected + seen * mean
        answers.append(seen)
    answers.append(mixed(later, glow) / kept - expected)
    scales = answer_scales()
    for c, value in enumerate(answers):
        coded = to_answer_code(value, scales[c])
        for j in range(BAND_ROWS):
            codes[pl.ds(c * BAND_ROWS + j, slabs, stride=message), :] = coded[
                :, j * LANES : (j + 1) * LANES
            ]
    answer_sent[...] = as_words(codes[...])

    def answer_copy(slab):
        return remote(
            answer_sent.at[rows_of(slab)],
            answer_got.at[rows_of(depth_at)],
            send_sem.at[1],
            recv_sem.at[1],
            "depth",
            slab,
        )

    def answer_start(k, _):
        half = blocks // 2
        block = lax.rem(my_block + k, half) + (k // half) * half
        for g in range(bands):
            slab = owner_at(block, g)

            @pl.when(slab != depth_at)
            def _():
                answer_copy(slab).start()

        return 0

    lax.fori_loop(0, blocks, answer_start, 0)
    answer_got[rows_of(depth_at), :] = answer_sent[rows_of(depth_at), :]

    for copy in (slice_up, slice_down, row_up, row_down):
        copy.wait()

    rim[...] = rim_got[...].astype(jnp.float32)

    @pl.when(rows_at == 0)
    def _():
        rim[0] = edge[0]

    @pl.when(rows_at == groups - 1)
    def _():
        rim[1] = edge[1]

    def smooth_block(block, _):
        lanes = lanes_of(block)
        row = lax.broadcasted_iota(jnp.int32, (rows, LANES), 0)

        def smooth_step(step, carry):
            low, centre = carry
            chunk = pl.ds(pl.multiple_of(step * UNROLL, UNROLL), UNROLL)
            above, below = (rim[0, chunk, lanes], rim[1, chunk, lanes])
            for u in range(UNROLL):
                z = step * UNROLL + u
                high = dens[block, z + 2].astype(jnp.float32)
                upper = jnp.where(row == 0, above[u : u + 1], pltpu.roll(centre, 1, axis=0))
                lower = jnp.where(
                    row == rows - 1, below[u : u + 1], pltpu.roll(centre, rows - 1, axis=0)
                )
                smooth_out[block, z] = (2.0 * smooth_weight) * (
                    (centre - low) + (centre - high) + (centre - upper) + (centre - lower)
                )
                low, centre = centre, high
            return low, centre

        first, last = (dens[block, 1], dens[block, slices])
        dens[block, 0] = jnp.where(depth_at == 0, first, slice_got[0, :, lanes])
        dens[block, slices + 1] = jnp.where(depth_at == slabs - 1, last, slice_got[1, :, lanes])
        start = (dens[block, 0].astype(jnp.float32), first.astype(jnp.float32))
        lax.fori_loop(0, slices // UNROLL, smooth_step, start)
        return 0

    lax.fori_loop(0, blocks, smooth_block, 0)

    pltpu.make_async_copy(partial_sent.at[others], partial_sent.at[others], send_sem.at[0]).wait()
    pltpu.make_async_copy(answer_sent.at[others], answer_sent.at[others], send_sem.at[1]).wait()
    pltpu.make_async_copy(answer_got.at[others], answer_got.at[others], recv_sem.at[1]).wait()
    answer_out[...] = answer_got[...]


def gradient_kernel(
    slices_total,
    colour_ref,
    lit_ref,
    through_ref,
    slope_ref,
    smooth_ref,
    mean_ref,
    answer_ref,
    dens_grad_hbm,
    colour_grad_hbm,
    dens_grad,
    colour_grad,
    dens_sem,
    colour_sem,
):
    blocks, slices, rows, _ = lit_ref.shape
    bands = rows // BAND_ROWS
    message = 4 * BAND_ROWS
    band_rows = blocks * message
    scales = answer_scales()

    def output_copies(block, start, count):
        some = pl.ds(start, count)
        lanes = pl.ds(pl.multiple_of(block * LANES, LANES), LANES)
        return (
            pltpu.make_async_copy(
                dens_grad.at[block, some], dens_grad_hbm.at[some, :, lanes], dens_sem.at[block]
            ),
            pltpu.make_async_copy(
                colour_grad.at[block, :, some],
                colour_grad_hbm.at[:, some, :, lanes],
                colour_sem.at[block],
            ),
        )

    def gradient_block(block, _):
        words = [
            as_floats(answer_ref[pl.ds(pl.multiple_of(g * band_rows + block * message, message), message), :])
            for g in range(bands)
        ]

        def answer(c):
            coded = [value[c * BAND_ROWS : (c + 1) * BAND_ROWS] for value in words]
            return from_answer_code(jnp.concatenate(coded, axis=0), scales[c])

        residual = [answer(c) for c in range(3)]
        whole = mean_ref[block, 3] * answer(3)
        for c in range(3):
            whole = whole + residual[c] * mean_ref[block, c]
        strong = [slices_total * value for value in residual]

        def gradient_step(step, remaining):
            for u in range(UNROLL):
                z = step * UNROLL + u
                lit = lit_ref[block, z]
                seen = jnp.zeros_like(lit)
                for c in range(3):
                    colour = colour_ref[block, c, z]
                    seen = seen + residual[c] * colour
                    colour_grad[block, c, z] = (strong[c] * lit) * (colour * (1.0 - colour))
                remaining = remaining - lit * seen
                dens_grad[block, z] = (
                    slope_ref[block, z] * (through_ref[block, z] * seen - remaining)
                    + smooth_ref[block, z]
                )
            for copy in output_copies(block, step * UNROLL, UNROLL):
                copy.start()
            return remaining

        lax.fori_loop(0, slices // UNROLL, gradient_step, whole)
        return 0

    lax.fori_loop(0, blocks, gradient_block, 0)

    def finish(block, _):
        for copy in output_copies(block, 0, slices):
            copy.wait()
        return 0

    lax.fori_loop(0, blocks, finish, 0)


def local(slabs, groups, density_raw, colour_raw, target, slab_rank):
    slices, rows, width = density_raw.shape
    blocks = width // LANES
    message = 4 * BAND_ROWS
    voxels = (slices, rows, width)
    blocked = (blocks, slices, rows, LANES)
    coloured = (blocks, 3, slices, rows, LANES)
    f32 = jnp.float32
    bf16 = jnp.bfloat16
    anywhere = pl.BlockSpec(memory_space=pl.ANY)
    vmem = pl.BlockSpec(memory_space=pltpu.VMEM)
    packet = pltpu.VMEM((slabs * message, LANES), jnp.int16)
    saved = pl.pallas_call(
        functools.partial(light_kernel, slabs, groups),
        out_shape=(
            pltpu.VMEM(coloured, f32),
            pltpu.VMEM(blocked, f32),
            pltpu.VMEM(blocked, f32),
            pltpu.VMEM(blocked, f32),
            pltpu.VMEM(blocked, f32),
            pltpu.VMEM((blocks, 4, rows, LANES), f32),
            packet,
        ),
        in_specs=[anywhere] * 4,
        out_specs=(vmem,) * 7,
        scratch_shapes=[
            pltpu.VMEM((blocks, slices + 2, rows, LANES), bf16),
            pltpu.VMEM(coloured, bf16),
            pltpu.VMEM((3, rows, LANES), f32),
            pltpu.VMEM((2, slices, width), f32),
            pltpu.VMEM((2, slices, width), bf16),
            pltpu.VMEM((2, slices, width), bf16),
            pltpu.VMEM((2, slices, width), f32),
            packet,
            packet,
            packet,
            packet,
            pltpu.VMEM((slabs * message, LANES), f32),
            pltpu.VMEM((2, rows, width), bf16),
            pltpu.SMEM((slabs,), jnp.int32),
            pltpu.SemaphoreType.DMA,
            pltpu.SemaphoreType.DMA((blocks,)),
            pltpu.SemaphoreType.DMA((blocks,)),
            pltpu.SemaphoreType.DMA,
            pltpu.SemaphoreType.DMA((2,)),
            pltpu.SemaphoreType.DMA((2,)),
            pltpu.SemaphoreType.DMA((4,)),
            pltpu.SemaphoreType.DMA((4,)),
        ],
        compiler_params=pltpu.CompilerParams(
            collective_id=0, has_side_effects=True, vmem_limit_bytes=40 * 2**20
        ),
        name="light",
    )(density_raw, colour_raw, target, slab_rank)
    return pl.pallas_call(
        functools.partial(gradient_kernel, float(slices * slabs)),
        out_shape=(
            jax.ShapeDtypeStruct(voxels, f32),
            jax.ShapeDtypeStruct((3, *voxels), f32),
        ),
        in_specs=[vmem] * 7,
        out_specs=(anywhere, anywhere),
        scratch_shapes=[
            pltpu.VMEM(blocked, f32),
            pltpu.VMEM(coloured, f32),
            pltpu.SemaphoreType.DMA((blocks,)),
            pltpu.SemaphoreType.DMA((blocks,)),
        ],
        compiler_params=pltpu.CompilerParams(vmem_limit_bytes=16 * 2**20),
        name="gradient",
    )(*saved)


def solution(mesh):
    return jax.shard_map(
        functools.partial(local, mesh.shape["depth"], mesh.shape["rows"]),
        mesh=mesh,
        in_specs=(P("depth", "rows", None), P(None, "depth", "rows", None), P(None, "rows", None), P()),
        out_specs=(P("depth", "rows", None), P(None, "depth", "rows", None)),
        check_vma=False,
    )
```
